256 devices in a mesh: ctx: 64 (over x, z, core), tp: 4 (over y).
Axes of the slice: x: 4, y: 4, z: 8, core: 2. Of those that a mesh axis runs over, the one named last changes fastest.
Arguments:
- hidden: bfloat16 [28672, 8192], P('ctx', 'tp'), may hold values from -14 to 14
- query_rows: bfloat16 [512, 4096], P('ctx', 'tp'), may hold values from -35 to 35
- query_weight: bfloat16 [8192, 4096], P('ctx', 'tp'), may hold values from -0.125 to 0.125
- key_weight: bfloat16 [8192, 512], P('ctx', 'tp'), may hold values from -0.0625 to 0.0625
- value_weight: bfloat16 [8192, 512], P('ctx', 'tp'), may hold values from -0.0625 to 0.0625
- query_down: bfloat16 [8192, 128], P('tp'), may hold values from -0.0625 to 0.0625
- value_down: bfloat16 [8192, 128], P('tp'), may hold values from -0.0625 to 0.0625
- query_up: bfloat16 [8, 16, 4096], P(None, None, 'tp'), may hold values from -1.5 to 1.5
- value_up: bfloat16 [8, 16, 512], P(None, None, 'tp'), may hold values from -1.5 to 1.5
- block_order: int32 [64], replicated, may hold values from 0 to 63, each once
- tenant: int32 [64], replicated, may hold values from 0 to 7
Outputs:
- context_out: bfloat16 [28672, 4096], P('ctx', 'tp')
- answer: bfloat16 [512, 4096], P('ctx', 'tp')
The draws below stay inside these ranges and needn't reach their ends.
All inputs are finite; a program needn't handle non-finite values.
Results may differ from the reference program's by a relative error of at most 0.028.
The reference program's roundings to bfloat16 on the way (of `weights`) count: a program that leaves them out, or rounds other values in their place, can miss the bound.
Values may be sent and summed in bfloat16 or wider, within the bound.
No kernel may reach another device: no remote copies, remote signals or barrier semaphores. Data moves between devices by JAX's collectives and lax.ppermute only.
A program may use at most 128 MiB of HBM per device.

```python
import jax
import jax.numpy as jnp
from jax import lax

D = 8192
HEADS = 32
KV_GROUPS = 4
HEAD = 128
RANK = 16
TENANTS = 8
BLOCK = 448
HOSTS = 64
CTX_TOK = 28672
QROWS = 512


def drawn_rows(key, row_count, col_count, amplitude):
    return jnp.clip(jax.random.normal(key, (row_count, col_count), jnp.float32), -6.0, 6.0) * amplitude


def draw_hidden(key, part):
    key = jax.random.fold_in(key, 11)
    values = drawn_rows(key, CTX_TOK, D, 1.0)
    return values.astype(jnp.bfloat16)


def draw_query_rows(key, part):
    key = jax.random.fold_in(key, 12)
    values = drawn_rows(key, QROWS, HEADS * HEAD, 2.5)
    return values.astype(jnp.bfloat16)


def with_ends(values, key, least, high):
    index_at = [jax.random.randint(jax.random.fold_in(key, axis), (), 0, length) for axis, length in enumerate(values.shape)]
    widest = values.shape.index(max(values.shape))
    beside = index_at[:widest] + [(index_at[widest] + 1) % values.shape[widest]] + index_at[widest + 1:]
    return values.at[tuple(index_at)].set(least).at[tuple(beside)].set(high)


def levels(stream_key, extent, cuts, smallest, largest):
    factor_of = 1.0
    for dim, shards_of in cuts:
        steps = jax.random.uniform(jax.random.fold_in(jax.random.fold_in(stream_key, 6), dim), (shards_of,), jnp.float32, smallest / len(cuts), largest / len(cuts))
        factor_of = factor_of * jnp.repeat(jnp.exp(steps), extent[dim] // shards_of).reshape((-1,) + (1,) * (len(extent) - 1 - dim))
    return factor_of


def gaussian(own_key, shape, deviation, limit, shards=(), kind=jnp.bfloat16):
    gain = levels(own_key, shape, shards, -0.22, 0.18) if shards else 1.0
    values = jax.random.normal(own_key, shape, jnp.float32) * deviation * gain
    return jnp.minimum(jnp.maximum(values, -limit), limit).astype(kind)


def setup_inputs(seed: int = 0) -> dict:
    key_list = jax.random.split(jax.random.key(seed), 12)
    hidden = draw_hidden(jax.random.fold_in(key_list[11], 71), 0)
    query_rows = draw_query_rows(jax.random.fold_in(key_list[11], 71), 0)
    query_weight = gaussian(key_list[2], (D, HEADS * HEAD), (D // 4) ** -0.5, 0.125, ((0, 64), (1, 4)))
    key_weight = gaussian(key_list[3], (D, KV_GROUPS * HEAD), D ** -0.5, 0.0625, ((0, 64), (1, 4)))
    value_weight = gaussian(key_list[4], (D, KV_GROUPS * HEAD), D ** -0.5, 0.0625, ((0, 64), (1, 4)))
    query_down = gaussian(key_list[5], (D, TENANTS * RANK), D ** -0.5, 0.0625, ((0, 4),))
    value_down = gaussian(key_list[6], (D, TENANTS * RANK), D ** -0.5, 0.0625, ((0, 4),))
    query_up = gaussian(key_list[7], (TENANTS, RANK, HEADS * HEAD), RANK ** -0.5, 1.5, ((2, 4),))
    value_up = gaussian(key_list[8], (TENANTS, RANK, KV_GROUPS * HEAD), RANK ** -0.5, 1.5, ((2, 4),))
    block_order = jax.random.permutation(key_list[9], HOSTS).astype(jnp.int32)
    tenant = with_ends(jax.random.randint(key_list[10], (HOSTS,), 0, TENANTS), jax.random.fold_in(key_list[10], 1), 0, TENANTS - 1).astype(jnp.int32)
    return {"hidden": hidden, "query_rows": query_rows, "query_weight": query_weight, "key_weight": key_weight, "value_weight": value_weight, "query_down": query_down, "value_down": value_down, "query_up": query_up, "value_up": value_up, "block_order": block_order, "tenant": tenant}


rope_base = 500000.0
masked = -1.0e30


def rotate(values, positions):
    half_size = HEAD // 2
    frequency = rope_base ** (-(jnp.arange(half_size, dtype=jnp.float32) / half_size))
    angles = positions.astype(jnp.float32)[:, None] * frequency[None, :]
    cosine = jnp.cos(angles)[:, None, :]
    sines = jnp.sin(angles)[:, None, :]
    shaped = values.reshape(values.shape[0], -1, HEAD)
    leading = shaped[..., :half_size]
    second = shaped[..., half_size:]
    turned = jnp.concatenate([leading * cosine - second * sines, second * cosine + leading * sines], axis=-1)
    return turned.reshape(values.shape)


def project(tokens, query_weight, key_weight, value_weight, query_down, value_down, query_up, value_up, owner_tenant, positions):
    start_col = (owner_tenant * RANK).astype(jnp.int32)
    low_query = jnp.dot(tokens, query_down, preferred_element_type=jnp.float32)
    low_value = jnp.dot(tokens, value_down, preferred_element_type=jnp.float32)
    picked_query = lax.dynamic_slice_in_dim(low_query, start_col, RANK, 1).astype(jnp.bfloat16)
    picked_value = lax.dynamic_slice_in_dim(low_value, start_col, RANK, 1).astype(jnp.bfloat16)
    lift_query = lax.dynamic_index_in_dim(query_up, owner_tenant.astype(jnp.int32), 0, keepdims=False)
    lift_value = lax.dynamic_index_in_dim(value_up, owner_tenant.astype(jnp.int32), 0, keepdims=False)
    queries = jnp.dot(tokens, query_weight, preferred_element_type=jnp.float32) + jnp.dot(picked_query, lift_query, preferred_element_type=jnp.float32)
    key_rows = jnp.dot(tokens, key_weight, preferred_element_type=jnp.float32)
    values = jnp.dot(tokens, value_weight, preferred_element_type=jnp.float32) + jnp.dot(picked_value, lift_value, preferred_element_type=jnp.float32)
    return rotate(queries, positions).astype(jnp.bfloat16), rotate(key_rows, positions).astype(jnp.bfloat16), values.astype(jnp.bfloat16)


def split_heads(queries, key_rows, values):
    row_count = queries.shape[0]
    group_count = key_rows.shape[1] // HEAD
    head_count = queries.shape[1] // HEAD
    query_split = queries.astype(jnp.float32).reshape(row_count, group_count, head_count // group_count, HEAD)
    key_split = key_rows.astype(jnp.float32).reshape(key_rows.shape[0], group_count, HEAD)
    value_split = values.astype(jnp.float32).reshape(values.shape[0], group_count, HEAD)
    return query_split, key_split, value_split


def context_attention(queries, key_rows, values, allowed):
    row_count = queries.shape[0]
    query_split, key_split, value_split = split_heads(queries, key_rows, values)
    scores = jnp.einsum("qgnd,kgd->gnqk", query_split, key_split) * (HEAD ** -0.5)
    scores = jnp.where(allowed[None, None], scores, masked)
    highest = jnp.max(scores, axis=-1, keepdims=True)
    weights = jnp.exp(scores - highest)
    weights = (weights / jnp.sum(weights, axis=-1, keepdims=True)).astype(jnp.bfloat16)
    mixed = jnp.einsum("gnqk,kgd->qgnd", weights.astype(jnp.float32), value_split)
    return mixed.reshape(row_count, queries.shape[1]).astype(jnp.bfloat16)


def partial_attention(queries, key_rows, values):
    row_count = queries.shape[0]
    head_count = queries.shape[1] // HEAD
    query_split, key_split, value_split = split_heads(queries, key_rows, values)
    scores = jnp.einsum("qgnd,kgd->gnqk", query_split, key_split) * (HEAD ** -0.5)
    highest = jnp.max(scores, axis=-1)
    weights = jnp.exp(scores - highest[..., None])
    totals = jnp.sum(weights, axis=-1)
    sum_terms = jnp.einsum("gnqk,kgd->qgnd", weights.astype(jnp.bfloat16).astype(jnp.float32), value_split)
    maxima = jnp.transpose(highest, (2, 0, 1)).reshape(row_count, head_count)
    totals = jnp.transpose(totals, (2, 0, 1)).reshape(row_count, head_count)
    return maxima, totals, sum_terms.reshape(row_count, head_count * HEAD)


def reference(hidden, query_rows, query_weight, key_weight, value_weight, query_down, value_down, query_up, value_up, block_order, tenant):
    host_count = block_order.shape[0]
    token_slabs = hidden.reshape(host_count, BLOCK, D)
    offsets = jnp.arange(BLOCK, dtype=jnp.int32)
    host_ids = jnp.arange(host_count, dtype=jnp.int32)

    def encode(host_index):
        block_id = block_order[host_index]
        owner_tenant = tenant[block_id]
        positions = block_id * BLOCK + offsets
        return project(token_slabs[host_index], query_weight, key_weight, value_weight, query_down, value_down, query_up, value_up, owner_tenant, positions)

    ctx_queries, key_cache, value_cache = lax.map(encode, host_ids)
    anchor_host = jnp.sum(host_ids * (block_order == 0).astype(jnp.int32))
    anchor_keys = key_cache[anchor_host]
    anchor_values = value_cache[anchor_host]
    causal = offsets[:, None] >= offsets[None, :]

    def attend(host_index):
        anchor_keep = jnp.broadcast_to(block_order[host_index] != 0, (BLOCK, BLOCK))
        allowed = jnp.concatenate([anchor_keep, causal], axis=1)
        joined_keys = jnp.concatenate([anchor_keys, key_cache[host_index]], axis=0)
        joined_values = jnp.concatenate([anchor_values, value_cache[host_index]], axis=0)
        return context_attention(ctx_queries[host_index], joined_keys, joined_values, allowed)

    context_out = lax.map(attend, host_ids).reshape(host_count * BLOCK, HEADS * HEAD)

    def track_max(running, host_index):
        maxima, _, _ = partial_attention(query_rows, key_cache[host_index], value_cache[host_index])
        return jnp.maximum(running, maxima), None

    initial = jnp.full((QROWS, HEADS), masked, dtype=jnp.float32)
    highest, _ = lax.scan(track_max, initial, host_ids)

    def add_terms(running, host_index):
        maxima, totals, sum_terms = partial_attention(query_rows, key_cache[host_index], value_cache[host_index])
        factor = jnp.exp(maxima - highest)
        return (running[0] + factor * totals, running[1] + jnp.repeat(factor, HEAD, axis=1) * sum_terms), None

    zero_totals = jnp.zeros((QROWS, HEADS), dtype=jnp.float32)
    zero_sums = jnp.zeros((QROWS, HEADS * HEAD), dtype=jnp.float32)
    (merged_totals, merged_sums), _ = lax.scan(add_terms, (zero_totals, zero_sums), host_ids)
    answer = (merged_sums / jnp.repeat(merged_totals, HEAD, axis=1)).astype(jnp.bfloat16)
    return context_out, answer
```

```python
import functools

import jax
import jax.numpy as jnp
from jax import lax
from jax.experimental import pallas as pl
from jax.experimental.pallas import tpu as pltpu
from jax.sharding import PartitionSpec as P

HEAD = 128
RANK = 16
XS, ZS, YS = 4, 8, 4
ROWS = 448
VMEM = 48 * 1024 * 1024
BF = jnp.bfloat16
F32 = jnp.float32

rope_base = 500000.0
masked = -1e30
scale = HEAD ** (-0.5)


def place(x, z, core):
    return (x % XS) * 16 + (z % ZS) * 2 + core


def ctx_move(value, dx=0, dz=0, swap=False):
    pairs = []
    for x in range(XS):
        for z in range(ZS):
            for core in range(2):
                pairs.append((place(x, z, core), place(x + dx, z + dz, 1 - core if swap else core)))
    return lax.ppermute(value, "ctx", pairs)


def swap_core(value):
    return ctx_move(value, swap=True)


def move_y(value, dy):
    return lax.ppermute(value, "tp", [(y, (y + dy) % YS) for y in range(YS)])


def ring(piece, count, forward, backward):
    pieces = [None] * count
    pieces[0] = piece
    ahead = behind = piece
    for step in range(1, count // 2):
        ahead, behind = forward(ahead), backward(behind)
        pieces[step], pieces[count - step] = ahead, behind
    half = piece.shape[0] // 2
    pieces[count // 2] = (forward(ahead[:half]), backward(behind[half:]))
    return pieces


def ordered(pieces, me):
    count = len(pieces)
    buffer = jnp.zeros((count,) + pieces[0].shape, pieces[0].dtype)
    zeros = (0,) * (pieces[0].ndim - 1)
    for back, piece in enumerate(pieces):
        at = lax.rem(me - back + count, count)
        if isinstance(piece, tuple):
            low, high = piece
            buffer = lax.dynamic_update_slice(buffer, low[None], (at, 0) + zeros)
            buffer = lax.dynamic_update_slice(buffer, high[None], (at, low.shape[0]) + zeros)
        else:
            buffer = lax.dynamic_update_slice(buffer, piece[None], (at, 0) + zeros)
    return buffer


def call(kernel, flops, moved, exps=0, **kw):
    return pl.pallas_call(
        kernel,
        compiler_params=pltpu.CompilerParams(vmem_limit_bytes=VMEM),
        cost_estimate=pl.CostEstimate(flops=flops, bytes_accessed=moved, transcendentals=exps),
        **kw,
    )


def parity_kernel(core_ref, hidden_ref, mine_ref, theirs_ref):
    first = core_ref[0] == 0
    for block in range(8):
        even = hidden_ref[:, block * 256 : block * 256 + 128]
        odd = hidden_ref[:, block * 256 + 128 : block * 256 + 256]
        mine_ref[:, block * 128 : block * 128 + 128] = jnp.where(first, even, odd)
        theirs_ref[:, block * 128 : block * 128 + 128] = jnp.where(first, odd, even)


def split_parity(hidden, core):
    shape = jax.ShapeDtypeStruct((ROWS, 1024), BF)
    return call(
        parity_kernel,
        0,
        4 * ROWS * 2048,
        out_shape=(shape, shape),
        in_specs=[pl.BlockSpec(memory_space=pltpu.SMEM), pl.BlockSpec(memory_space=pltpu.VMEM)],
        out_specs=(pl.BlockSpec(memory_space=pltpu.VMEM),) * 2,
    )(core.reshape(1), hidden)


def project_kernel(tokens_ref, weight_ref, out_ref):
    product = jnp.dot(tokens_ref[0], weight_ref[0], preferred_element_type=F32)

    @pl.when(pl.program_id(0) == 0)
    def _():
        out_ref[...] = product

    @pl.when(pl.program_id(0) > 0)
    def _():
        out_ref[...] += product


def project(tokens, weight):
    parts, rows, depth = tokens.shape
    cols = weight.shape[2]
    return call(
        project_kernel,
        2 * parts * rows * depth * cols,
        2 * parts * depth * (rows + cols) + 4 * rows * cols,
        out_shape=jax.ShapeDtypeStruct((rows, cols), F32),
        grid=(parts,),
        in_specs=[
            pl.BlockSpec((1, rows, depth), lambda i: (i, 0, 0)),
            pl.BlockSpec((1, depth, cols), lambda i: (i, 0, 0)),
        ],
        out_specs=pl.BlockSpec((rows, cols), lambda i: (0, 0)),
    )(tokens, weight)


def turn(values, cosine, sine):
    return values * cosine + pltpu.roll(values, HEAD // 2, 1) * sine


def keys_kernel(own_ref, got_ref, lift_ref, cos_ref, sin_ref, out_ref):
    keys = own_ref[:, :HEAD] + got_ref[:, :HEAD]
    out_ref[:, :HEAD] = turn(keys, cos_ref[...], sin_ref[...]).astype(BF)
    values = own_ref[:, HEAD:] + got_ref[:, HEAD:]
    out_ref[:, HEAD:] = (values + lift_ref[...]).astype(BF)


def finish_keys(own, got, lift, cosine, sine):
    wide = pl.BlockSpec((ROWS, 256), lambda i: (0, 0))
    thin = pl.BlockSpec((ROWS, 128), lambda i: (0, 0))
    return call(
        keys_kernel,
        0,
        ROWS * 128 * 32,
        out_shape=jax.ShapeDtypeStruct((ROWS, 256), BF),
        grid=(1,),
        in_specs=[wide, wide, thin, thin, thin],
        out_specs=wide,
    )(own, got, lift, cosine, sine)


def against(queries, keys):
    return lax.dot_general(queries, keys, (((1,), (1,)), ((), ())), preferred_element_type=F32) * scale


def context_kernel(first_ref, own_ref, got_ref, lift_ref, cos_ref, sin_ref, pair_ref, anchor_ref, *rest):
    out_ref = rest[-1]
    queries = own_ref[...] + got_ref[...] + lift_ref[...]
    queries = turn(queries, cos_ref[...], sin_ref[...]).astype(BF)
    to_anchor = against(queries, anchor_ref[:, :HEAD])
    to_anchor = jnp.where(first_ref[0] == 0, masked, to_anchor)
    to_own = against(queries, pair_ref[:, :HEAD])
    row = lax.broadcasted_iota(jnp.int32, (ROWS, ROWS), 0)
    col = lax.broadcasted_iota(jnp.int32, (ROWS, ROWS), 1)
    to_own = jnp.where(row >= col, to_own, masked)
    highest = jnp.maximum(
        jnp.max(to_anchor, axis=1, keepdims=True), jnp.max(to_own, axis=1, keepdims=True)
    )
    to_anchor = jnp.exp(to_anchor - highest)
    to_own = jnp.exp(to_own - highest)
    total = jnp.sum(to_anchor, axis=1, keepdims=True) + jnp.sum(to_own, axis=1, keepdims=True)
    share = 1.0 / total
    mixed = jnp.dot((to_anchor * share).astype(BF), anchor_ref[:, HEAD:], preferred_element_type=F32)
    mixed += jnp.dot((to_own * share).astype(BF), pair_ref[:, HEAD:], preferred_element_type=F32)
    out_ref[...] = mixed.astype(BF)


def context_attention(block_id, own, got, lift, cosine, sine, pair, anchor, heads, skip, at, before=None):
    wide = pl.BlockSpec((ROWS, 256), lambda h: (0, 0))
    thin = pl.BlockSpec((ROWS, 128), lambda h: (0, 0))
    specs = [
        pl.BlockSpec(memory_space=pltpu.SMEM),
        pl.BlockSpec((ROWS, 128), lambda h: (0, h + skip)),
        pl.BlockSpec((ROWS, 128), lambda h: (0, h + skip)),
        pl.BlockSpec((ROWS, 128), lambda h: (0, h + at)),
        thin,
        thin,
        wide,
        wide,
    ]
    args = [block_id.reshape(1), own, got, lift, cosine, sine, pair, anchor]
    alias = {}
    if before is not None:
        specs.append(pl.BlockSpec(memory_space=pl.ANY))
        args.append(before)
        alias = {8: 0}
    return call(
        context_kernel,
        heads * 8 * ROWS * ROWS * HEAD,
        heads * ROWS * 128 * 16,
        heads * ROWS * ROWS * 2,
        out_shape=jax.ShapeDtypeStruct((ROWS, 1024), BF),
        grid=(heads,),
        in_specs=specs,
        out_specs=pl.BlockSpec((ROWS, 128), lambda h: (0, h + at)),
        input_output_aliases=alias,
    )(*args)


def query_kernel(query_ref, pair_ref, out_ref, stats_ref):
    head = pl.program_id(0)
    scores = against(query_ref[...], pair_ref[:, :HEAD])
    highest = jnp.max(scores, axis=1, keepdims=True)
    weights = jnp.exp(scores - highest)
    total = jnp.sum(weights, axis=1, keepdims=True)
    out_ref[...] = jnp.dot(weights.astype(BF), pair_ref[:, HEAD:], preferred_element_type=F32)

    @pl.when(head == 0)
    def _():
        stats_ref[...] = jnp.zeros_like(stats_ref)

    lane = lax.broadcasted_iota(jnp.int32, stats_ref.shape, 1)
    kept = jnp.where(lane == head, highest, stats_ref[...])
    stats_ref[...] = jnp.where(lane == head + 8, total, kept)


def query_attention(queries, pair):
    rows = queries.shape[0]
    block = pl.BlockSpec((rows, 128), lambda h: (0, h))
    return call(
        query_kernel,
        8 * 4 * rows * ROWS * HEAD,
        rows * 1024 * 6,
        8 * rows * ROWS,
        out_shape=(jax.ShapeDtypeStruct((rows, 1024), F32), jax.ShapeDtypeStruct((rows, 128), F32)),
        grid=(8,),
        in_specs=[block, pl.BlockSpec((ROWS, 256), lambda h: (0, 0))],
        out_specs=(block, pl.BlockSpec((rows, 128), lambda h: (0, 0))),
    )(queries, pair)


def merge_kernel(count, last, *refs):
    sums, stats = refs[:count], refs[count : 2 * count]
    stat = [ref[...] for ref in stats]
    lane = lax.broadcasted_iota(jnp.int32, stat[0].shape, 1)
    highest = functools.reduce(jnp.maximum, stat)
    factors = [jnp.exp(jnp.where(lane < 8, one - highest, 0.0)) for one in stat]
    totals = sum(one * pltpu.roll(factor, 8, 1) for one, factor in zip(stat, factors))
    for head in range(8):
        cols = slice(head * HEAD, (head + 1) * HEAD)
        merged = sum(
            ref[:, cols].astype(F32) * factor[:, head : head + 1] for ref, factor in zip(sums, factors)
        )
        if last:
            refs[-1][:, cols] = (merged / totals[:, head + 8 : head + 9]).astype(BF)
        else:
            refs[-2][:, cols] = merged.astype(refs[-2].dtype)
    if not last:
        refs[-1][...] = jnp.where(lane < 8, highest, totals)


def merge(sums, stats, dtype, last=False):
    rows = sums[0].shape[0]
    count = len(sums)
    out = jax.ShapeDtypeStruct((rows, 1024), dtype)
    shapes = out if last else (out, jax.ShapeDtypeStruct((rows, 128), F32))
    vmem = pl.BlockSpec(memory_space=pltpu.VMEM)
    return call(
        functools.partial(merge_kernel, count, last),
        0,
        (count + 1) * rows * 1152 * 4,
        out_shape=shapes,
        in_specs=[vmem] * (2 * count),
        out_specs=vmem if last else (vmem, vmem),
    )(*sums, *stats)


def exchange(value, me, count, move):
    got = [lax.dynamic_index_in_dim(value, me, 0, keepdims=False)]
    for step in range(1, count):
        at = lax.rem(me + step, count)
        got.append(move(lax.dynamic_index_in_dim(value, at, 0, keepdims=False), step))
    return got


def shards(
    hidden,
    query_rows,
    query_weight,
    key_weight,
    value_weight,
    query_down,
    value_down,
    query_up,
    value_up,
    block_order,
    tenant,
):
    my_index = lax.axis_index("ctx")
    x, z, core = my_index // 16, lax.rem(my_index // 2, ZS), lax.rem(my_index, 2)
    y = lax.axis_index("tp")
    host_ids = jnp.arange(64, dtype=jnp.int32)
    block_id = jnp.sum(jnp.where(host_ids == my_index, block_order, 0))
    owner = jnp.sum(jnp.where(host_ids == block_id, tenant, 0))

    all_queries = lax.all_gather(query_rows, "ctx", axis=0, tiled=True)

    z_first = jnp.concatenate([key_weight, value_weight, query_weight[:, :384]], axis=1)
    x_first = query_weight[:, 384:]
    fx, bx = (lambda v: ctx_move(v, dx=1)), (lambda v: ctx_move(v, dx=-1))
    fz, bz = (lambda v: ctx_move(v, dz=1)), (lambda v: ctx_move(v, dz=-1))

    mine, theirs = split_parity(hidden, core)
    other = swap_core(theirs)
    own_parts, other_parts = [mine], [other]
    for _ in range(3):
        own_parts.append(move_y(own_parts[-1], 1))
        other_parts.append(move_y(other_parts[-1], -1))
    own_tokens = ordered(own_parts, y)
    other_tokens = ordered([other_parts[0]] + other_parts[:0:-1], y)

    z_line = ordered(ring(z_first, ZS, fz, bz), z)
    x_line = ordered(ring(x_first, XS, fx, bx), x)
    z_weight = ordered(ring(z_line, XS, fx, bx), x).reshape(XS, 1024, 640)
    x_pieces = ring(x_line, ZS, fz, bz)
    x_weight = jnp.zeros((XS, ZS, 128, 640), BF)
    for back, piece in enumerate(x_pieces):
        at = lax.rem(z - back + ZS, ZS)
        if isinstance(piece, tuple):
            x_weight = lax.dynamic_update_slice(x_weight, piece[0][:, None], (0, at, 0, 0))
            x_weight = lax.dynamic_update_slice(x_weight, piece[1][:, None], (XS // 2, at, 0, 0))
        else:
            x_weight = lax.dynamic_update_slice(x_weight, piece[:, None], (0, at, 0, 0))
    x_weight = x_weight.reshape(XS, 1024, 640)

    down = jnp.concatenate(
        [
            lax.dynamic_slice_in_dim(query_down, owner * RANK, RANK, 1),
            lax.dynamic_slice_in_dim(value_down, owner * RANK, RANK, 1),
        ],
        axis=1,
    )
    low = lax.dot_general(down, hidden, (((0,), (1,)), ((), ())), preferred_element_type=F32)
    low = low + lax.ppermute(low, "tp", [(i, i ^ 1) for i in range(YS)])
    low = low + lax.ppermute(low, "tp", [(i, i ^ 2) for i in range(YS)])
    low = low.astype(BF)
    over_rank = (((0,), (0,)), ((), ()))
    query_lift = lax.dot_general(
        low[:RANK], lax.dynamic_index_in_dim(query_up, owner, 0, keepdims=False), over_rank, preferred_element_type=F32
    )
    value_lift = lax.dot_general(
        low[RANK:], lax.dynamic_index_in_dim(value_up, owner, 0, keepdims=False), over_rank, preferred_element_type=F32
    )
    half = HEAD // 2
    positions = block_id * ROWS + jnp.arange(ROWS, dtype=jnp.int32)
    frequency = rope_base ** (-(jnp.arange(half, dtype=F32) / half))
    angles = positions.astype(F32)[:, None] * frequency[None, :]
    cosine, sine = jnp.cos(angles), jnp.sin(angles)
    cosine = jnp.concatenate([cosine, cosine], axis=1)
    sine = jnp.concatenate([-sine, sine], axis=1)

    got_z = swap_core(project(other_tokens, z_weight))
    own_z = project(own_tokens, z_weight)
    got_x = swap_core(project(other_tokens, x_weight))
    own_x = project(own_tokens, x_weight)
    pair = finish_keys(own_z, got_z, value_lift, cosine, sine)

    kept = jnp.where(block_id == 0, pair, jnp.zeros_like(pair))
    kept = kept + swap_core(kept)
    half_pair = jnp.where(core == 0, kept[:, :HEAD], kept[:, HEAD:])
    half_pair = half_pair + fz(half_pair) + bz(half_pair)
    up3, down3 = ctx_move(half_pair, dz=3), ctx_move(half_pair, dz=-3)
    half_pair = jnp.where(half_pair != 0, half_pair, jnp.where(up3 != 0, up3, down3))
    half_pair = half_pair + fx(half_pair) + bx(half_pair) + ctx_move(half_pair, dx=2)
    other_half = swap_core(half_pair)
    anchor = jnp.concatenate(
        [jnp.where(core == 0, half_pair, other_half), jnp.where(core == 0, other_half, half_pair)], axis=1
    )

    sums, stats = query_attention(all_queries, pair)
    sums = sums.reshape(32, 2, 8, 1024)
    stats = stats.reshape(32, 2, 8, 128)

    def part(value, at, lanes):
        return lax.dynamic_index_in_dim(value, at, 1, keepdims=False).reshape(256, lanes)

    sums, stats = merge(
        [part(sums, core, 1024), swap_core(part(sums, 1 - core, 1024))],
        [part(stats, core, 128), swap_core(part(stats, 1 - core, 128))],
        BF,
    )
    along_x = lambda v, k: ctx_move(v, dx=k)
    along_z = lambda v, k: ctx_move(v, dz=k)
    sums, stats = merge(
        exchange(sums.reshape(XS, 64, 1024), x, XS, along_x),
        exchange(stats.reshape(XS, 64, 128), x, XS, along_x),
        F32,
    )
    answer = merge(
        exchange(sums.reshape(ZS, 8, 1024), z, ZS, along_z),
        exchange(stats.reshape(ZS, 8, 128), z, ZS, along_z),
        BF,
        last=True,
    )

    context = context_attention(block_id, own_z, got_z, query_lift, cosine, sine, pair, anchor, 3, 2, 0)
    context = context_attention(block_id, own_x, got_x, query_lift, cosine, sine, pair, anchor, 5, 0, 3, context)
    return (context, answer)


def solution(mesh):
    placed = (
        P("ctx", "tp"),
        P("ctx", "tp"),
        P("ctx", "tp"),
        P("ctx", "tp"),
        P("ctx", "tp"),
        P("tp", None),
        P("tp", None),
        P(None, None, "tp"),
        P(None, None, "tp"),
        P(),
        P(),
    )
    return jax.shard_map(
        shards,
        mesh=mesh,
        in_specs=placed,
        out_specs=(P("ctx", "tp"), P("ctx", "tp")),
        check_vma=False,
    )
```

```python
import functools

import jax
import jax.numpy as jnp
from jax import lax
from jax.experimental import pallas as pl
from jax.experimental.pallas import tpu as pltpu
from jax.sharding import PartitionSpec as P

HEAD = 128
RANK = 16
XS, ZS, YS = 4, 8, 4
CORE, Z1, Z2, Z4, X1, X2 = 1, 2, 4, 8, 16, 32
LINE_SENT = 256
LINE = 192
AROUND, BLOCK_ID, CORE_AT, PLACE_X, OWNER, FLAGS = 0, 1, 2, 3, 4, 5
ROWS = 448
VMEM = 32 * 1024 * 1024
BF = jnp.bfloat16
F32 = jnp.float32

rope_base = 500000.0
masked = -1e30
scale = HEAD ** (-0.5)
power = scale * 1.4426950408889634


def place(x, z, core):
    return (x % XS) * 16 + (z % ZS) * 2 + core


def ctx_move(value, dx=0, dz=0, swap=False):
    pairs = []
    for x in range(XS):
        for z in range(ZS):
            for core in range(2):
                pairs.append((place(x, z, core), place(x + dx, z + dz, 1 - core if swap else core)))
    return lax.ppermute(value, "ctx", pairs)


def ctx_flip(value, bit):
    return lax.ppermute(value, "ctx", [(i, i ^ bit) for i in range(64)])


def swap_core(value):
    return ctx_move(value, swap=True)


def gather_z(value):
    lines = [[place(x, z, core) for z in range(ZS)] for x in range(XS) for core in range(2)]
    return lax.all_gather(value, "ctx", axis_index_groups=lines, axis=0, tiled=True)


def move_y(value, dy):
    return lax.ppermute(value, "tp", [(y, (y + dy) % YS) for y in range(YS)])


def ring(piece, count, forward, backward):
    pieces = [None] * count
    pieces[0] = piece
    ahead = behind = piece
    for step in range(1, count // 2):
        ahead, behind = forward(ahead), backward(behind)
        pieces[step], pieces[count - step] = ahead, behind
    half = piece.shape[0] // 2
    pieces[count // 2] = (forward(ahead[:half]), backward(behind[half:]))
    return pieces


def ordered(pieces, me):
    count = len(pieces)
    buffer = jnp.zeros((count,) + pieces[0].shape, pieces[0].dtype)
    zeros = (0,) * (pieces[0].ndim - 1)
    for back, piece in enumerate(pieces):
        at = lax.rem(me - back + count, count)
        if isinstance(piece, tuple):
            low, high = piece
            buffer = lax.dynamic_update_slice(buffer, low[None], (at, 0) + zeros)
            buffer = lax.dynamic_update_slice(buffer, high[None], (at, low.shape[0]) + zeros)
        else:
            buffer = lax.dynamic_update_slice(buffer, piece[None], (at, 0) + zeros)
    return buffer


def call(kernel, flops, moved, exps=0, **kw):
    return pl.pallas_call(
        kernel,
        compiler_params=pltpu.CompilerParams(vmem_limit_bytes=VMEM),
        cost_estimate=pl.CostEstimate(flops=flops, bytes_accessed=moved, transcendentals=exps),
        **kw,
    )


def parity_kernel(core_ref, hidden_ref, mine_ref, theirs_ref):
    first = core_ref[0] == 0
    for block in range(8):
        even = hidden_ref[:, block * 256 : block * 256 + 128]
        odd = hidden_ref[:, block * 256 + 128 : block * 256 + 256]
        mine_ref[:, block * 128 : block * 128 + 128] = jnp.where(first, even, odd)
        theirs_ref[:, block * 128 : block * 128 + 128] = jnp.where(first, odd, even)


def split_parity(core, hidden):
    shape = jax.ShapeDtypeStruct((ROWS, 1024), BF)
    return call(
        parity_kernel,
        0,
        4 * ROWS * 2048,
        out_shape=(shape, shape),
        in_specs=[pl.BlockSpec(memory_space=pltpu.SMEM), pl.BlockSpec(memory_space=pltpu.VMEM)],
        out_specs=(pl.BlockSpec(memory_space=pltpu.VMEM),) * 2,
    )(core.reshape(1), hidden)


def low_kernel(number_ref, hidden_ref, query_ref, value_ref, out_ref):
    shift = number_ref[OWNER] * RANK
    low_q = jnp.dot(hidden_ref[...], query_ref[...], preferred_element_type=F32)
    low_v = jnp.dot(hidden_ref[...], value_ref[...], preferred_element_type=F32)
    low_q = pltpu.roll(low_q, lax.rem(128 - shift, 128), 1)
    low_v = pltpu.roll(low_v, lax.rem(128 + RANK - shift, 128), 1)
    lane = lax.broadcasted_iota(jnp.int32, low_q.shape, 1)
    out_ref[...] = jnp.where(lane < RANK, low_q, low_v).T[: 2 * RANK]


def low_parts(numbers, hidden, query_down, value_down):
    vmem = pl.BlockSpec(memory_space=pltpu.VMEM)
    return call(
        low_kernel,
        2 * ROWS * 2048 * 256,
        2 * 2048 * (ROWS + 256),
        out_shape=jax.ShapeDtypeStruct((2 * RANK, ROWS), F32),
        in_specs=[pl.BlockSpec(memory_space=pltpu.SMEM)] + [vmem] * 3,
        out_specs=vmem,
    )(numbers, hidden, query_down, value_down)


def both(step, own_refs, other_refs):
    return jnp.concatenate([own_refs[step][...], other_refs[(YS - step) % YS][...]], axis=0)


def project_kernel(number_ref, *refs):
    own_refs, other_refs, weight_ref, own_out, other_out = refs[:4], refs[4:8], refs[8], refs[9], refs[10]
    for tile in range(own_out.shape[1] // 256):
        cols = slice(tile * 256, tile * 256 + 256)
        sums = None
        for step in range(YS):
            at = lax.rem(number_ref[AROUND] + step, YS)
            if weight_ref.shape[0] == XS:
                blocks = [weight_ref[at, block, :128, cols] for block in range(ZS)]
            else:
                blocks = [weight_ref[block, at, :, cols] for block in range(ZS)]
            product = jnp.dot(
                both(step, own_refs, other_refs), jnp.concatenate(blocks, axis=0), preferred_element_type=F32
            )
            sums = product if sums is None else sums + product
        own_out[:, cols] = sums[:ROWS]
        other_out[:, cols] = sums[ROWS:]


def project(numbers, own, other, weight):
    cols = weight.shape[-1]
    out = jax.ShapeDtypeStruct((ROWS, cols), F32)
    vmem = pl.BlockSpec(memory_space=pltpu.VMEM)
    return call(
        project_kernel,
        4 * ROWS * 4096 * cols,
        2 * 4096 * (2 * ROWS + cols) + 8 * ROWS * cols,
        out_shape=(out, out),
        in_specs=[pl.BlockSpec(memory_space=pltpu.SMEM)] + [vmem] * 9,
        out_specs=(vmem, vmem),
    )(numbers, *own, *other, weight)


def turn(values, cosine, sine):
    return values * cosine + pltpu.roll(values, HEAD // 2, 1) * sine


def keys_kernel(own_ref, got_ref, lift_ref, cos_ref, sin_ref, out_ref):
    keys = own_ref[:, :HEAD] + got_ref[:, :HEAD]
    out_ref[:, :HEAD] = turn(keys, cos_ref[...], sin_ref[...]).astype(BF)
    values = own_ref[:, HEAD:] + got_ref[:, HEAD:]
    out_ref[:, HEAD:] = (values + lift_ref[...]).astype(BF)


def finish_keys(own, got, lift, cosine, sine):
    return call(
        keys_kernel,
        ROWS * 128 * 8,
        ROWS * 128 * 32,
        out_shape=jax.ShapeDtypeStruct((ROWS, 256), BF),
        in_specs=[pl.BlockSpec(memory_space=pltpu.VMEM)] * 5,
        out_specs=pl.BlockSpec(memory_space=pltpu.VMEM),
    )(own, got, lift, cosine, sine)


def against(queries, keys):
    return lax.dot_general(queries, keys, (((1,), (1,)), ((), ())), preferred_element_type=F32)


def attend(queries, first, pair_ref, anchor_ref):
    to_anchor = against(queries, anchor_ref[:, :HEAD])
    to_anchor = jnp.where(first, masked, to_anchor)
    to_own = against(queries, pair_ref[:, :HEAD])
    row = lax.broadcasted_iota(jnp.int32, (ROWS, ROWS), 0)
    col = lax.broadcasted_iota(jnp.int32, (ROWS, ROWS), 1)
    to_own = jnp.where(row >= col, to_own, masked)
    highest = jnp.maximum(
        jnp.max(to_anchor, axis=1, keepdims=True), jnp.max(to_own, axis=1, keepdims=True)
    )
    to_anchor = jnp.exp2((to_anchor - highest) * power)
    to_own = jnp.exp2((to_own - highest) * power)
    total = jnp.sum(to_anchor, axis=1, keepdims=True) + jnp.sum(to_own, axis=1, keepdims=True)
    share = 1.0 / total
    mixed = jnp.dot((to_anchor * share).astype(BF), anchor_ref[:, HEAD:], preferred_element_type=F32)
    return mixed + jnp.dot((to_own * share).astype(BF), pair_ref[:, HEAD:], preferred_element_type=F32)


def unpacked(group_ref):
    return jnp.concatenate([group_ref[:, g * HEAD : (g + 1) * HEAD] for g in range(7)], axis=0)


def context_kernel(
    number_ref, own_ref, got_ref, lift_ref, cos_ref, sin_ref, pair_ref, mine_ref, theirs_ref, out_ref, anchor_ref
):
    @pl.when(pl.program_id(0) == 0)
    def _():
        mine, theirs = unpacked(mine_ref), unpacked(theirs_ref)
        anchor_ref[:, :HEAD] = jnp.where(number_ref[CORE_AT] == 0, mine, theirs)
        anchor_ref[:, HEAD:] = jnp.where(number_ref[CORE_AT] == 0, theirs, mine)

    queries = own_ref[...] + got_ref[...] + lift_ref[...]
    for head in range(2):
        cols = slice(head * HEAD, (head + 1) * HEAD)
        turned = turn(queries[:, cols], cos_ref[...], sin_ref[...]).astype(BF)
        out_ref[:, cols] = attend(turned, number_ref[BLOCK_ID] == 0, pair_ref, anchor_ref).astype(BF)


def context_attention(numbers, own, got, lift, cosine, sine, pair, mine, theirs):
    wide = pl.BlockSpec((ROWS, 256), lambda i: (0, 0))
    thin = pl.BlockSpec((ROWS, 128), lambda i: (0, 0))
    heads = pl.BlockSpec((ROWS, 256), lambda i: (0, i))
    packed = pl.BlockSpec((64, 1152), lambda i: (0, 0))
    return call(
        context_kernel,
        64 * ROWS * ROWS * HEAD,
        ROWS * 1024 * 14,
        16 * ROWS * ROWS,
        out_shape=jax.ShapeDtypeStruct((ROWS, 1024), BF),
        grid=(4,),
        in_specs=[pl.BlockSpec(memory_space=pltpu.SMEM), heads, heads, heads, thin, thin, wide, packed, packed],
        out_specs=heads,
        scratch_shapes=[pltpu.VMEM((ROWS, 256), BF)],
    )(numbers, own, got, lift, cosine, sine, pair, mine, theirs)


def pack_stats(stats):
    high = stats.astype(BF).astype(F32)
    rest = stats - high
    middle = rest.astype(BF).astype(F32)
    low = rest - middle
    return high + pltpu.roll(middle, 16, 1) + pltpu.roll(low, 32, 1)


def unpack_stats(group):
    terms = group.astype(F32)
    return terms + pltpu.roll(terms, 112, 1) + pltpu.roll(terms, 96, 1)


def stats_of(maxima, totals):
    rows = maxima[0].shape[0]
    lane = lax.broadcasted_iota(jnp.int32, (rows, 128), 1)
    stats = jnp.zeros((rows, 128), F32)
    for at, column in enumerate(maxima + totals):
        stats = jnp.where(lane == at, column, stats)
    return stats


def put(keep_ref, send_ref, top, cols, value, group, flag, stats=False):
    half = value.shape[0] // 2
    split = value.reshape(half // group, 2, group, value.shape[1])
    low, high = split[:, 0].reshape(half, -1), split[:, 1].reshape(half, -1)
    keep_ref[:, cols] = jnp.where(flag, high, low)
    sent = jnp.where(flag, low, high)
    if stats:
        sent = pack_stats(sent)
    if half < 16:
        sent = jnp.concatenate([sent, sent], axis=0)
    send_ref[top:, cols] = sent.astype(BF)


def query_kernel(number_ref, lines_ref, pair_ref, keep_ref, send_ref, query_ref):
    for side in range(2):
        for at_x in range(XS):
            back = lax.rem(number_ref[PLACE_X] + XS - at_x, XS)
            for pair in range(4):
                rows = []
                for place in (2 * pair, 2 * pair + 1):
                    block = lines_ref[back, place, 128 + 32 * side : 160 + 32 * side].astype(F32)
                    rows.append(jnp.concatenate([block[8 * g : 8 * g + 8] for g in range(4)], axis=1))
                at = 256 * side + 64 * at_x + 16 * pair
                query_ref[at : at + 16] = jnp.concatenate(rows, axis=0).astype(BF)

    send_ref[:128, 896:] = jnp.zeros((128, 256), BF)
    for half in range(2):
        cols = slice(half * HEAD, (half + 1) * HEAD)
        for g in range(7):
            piece = pair_ref[g * 64 : g * 64 + 64, cols]
            send_ref[half * 64 : half * 64 + 64, g * HEAD : (g + 1) * HEAD] = jnp.where(
                number_ref[BLOCK_ID] == 0, piece, jnp.zeros_like(piece)
            )
    rows = query_ref.shape[0]
    maxima, totals = [], []
    for head in range(8):
        cols = slice(head * HEAD, (head + 1) * HEAD)
        scores = against(query_ref[:, cols], pair_ref[:, :HEAD])
        highest = jnp.max(scores, axis=1, keepdims=True)
        weights = jnp.exp2((scores - highest) * power)
        maxima.append(highest * scale)
        totals.append(jnp.sum(weights, axis=1, keepdims=True))
        sums = jnp.dot(weights.astype(BF), pair_ref[:, HEAD:], preferred_element_type=F32)
        put(keep_ref, send_ref, 128, cols, sums, rows // 2, False)
    put(keep_ref, send_ref, 128, slice(1024, 1152), stats_of(maxima, totals), rows // 2, False, True)


def merge_kernel(group, at_flag, number_ref, mine_ref, sent_ref, got_ref, *out):
    flag = number_ref[at_flag] == 1
    rows = mine_ref.shape[0]
    top = 64 if rows < 256 else 128
    anchor = sent_ref[:top] + got_ref[:top]
    if top == 128:
        anchor = jnp.where(number_ref[CORE_AT] == 0, anchor[:64], anchor[64:])
    out[1][:64] = anchor
    lane = lax.broadcasted_iota(jnp.int32, (rows, 128), 1)
    one, two = mine_ref[:, 1024:], unpack_stats(got_ref[top:, 1024:])[:rows]
    highest = jnp.maximum(one, two)
    left = jnp.exp(jnp.where(lane < 8, one - highest, 0.0))
    right = jnp.exp(jnp.where(lane < 8, two - highest, 0.0))
    totals = one * pltpu.roll(left, 8, 1) + two * pltpu.roll(right, 8, 1)
    for head in range(8):
        cols = slice(head * HEAD, (head + 1) * HEAD)
        at = slice(head, head + 1)
        other = got_ref[top:, cols].astype(F32)[:rows]
        merged = mine_ref[:, cols] * left[:, at] + other * right[:, at]
        if group is None:
            out[0][:, cols] = (merged / totals[:, head + 8 : head + 9]).astype(BF)
        else:
            put(out[0], out[1], 64, cols, merged, group, flag)
    if group is not None:
        stats = jnp.where(lane < 8, highest, jnp.where(lane < 16, totals, 0.0))
        put(out[0], out[1], 64, slice(1024, 1152), stats, group, flag, True)


VMEM_BLOCK = pl.BlockSpec(memory_space=pltpu.VMEM)


def query_attention(numbers, lines, pair):
    rows = 512
    return call(
        query_kernel,
        32 * rows * ROWS * HEAD,
        rows * 1024 * 6,
        8 * rows * ROWS,
        out_shape=(
            jax.ShapeDtypeStruct((rows // 2, 1152), F32),
            jax.ShapeDtypeStruct((128 + rows // 2, 1152), BF),
        ),
        in_specs=[pl.BlockSpec(memory_space=pltpu.SMEM)] + [VMEM_BLOCK] * 2,
        out_specs=(VMEM_BLOCK,) * 2,
        scratch_shapes=[pltpu.VMEM((rows, 1024), BF)],
    )(numbers, lines, pair)


def merge(numbers, mine, sent, got, at_flag=0, group=None):
    rows = mine.shape[0]
    if group is None:
        shapes = (jax.ShapeDtypeStruct((rows, 1024), BF), jax.ShapeDtypeStruct((64, 1152), BF))
    else:
        half = rows // 2
        shapes = (
            jax.ShapeDtypeStruct((half, 1152), F32),
            jax.ShapeDtypeStruct((64 + max(half, 16), 1152), BF),
        )
    return call(
        functools.partial(merge_kernel, group, at_flag),
        8 * rows * 1024,
        rows * 1152 * 8,
        out_shape=shapes,
        in_specs=[pl.BlockSpec(memory_space=pltpu.SMEM)] + [VMEM_BLOCK] * 3,
        out_specs=(VMEM_BLOCK,) * 2,
    )(numbers, mine, sent, got)


def tie(*values):
    return lax.optimization_barrier(values)


def doubled(piece, bit_set, got):
    return jnp.concatenate([jnp.where(bit_set, got, piece), jnp.where(bit_set, piece, got)], axis=0)


def shards(
    hidden,
    query_rows,
    query_weight,
    key_weight,
    value_weight,
    query_down,
    value_down,
    query_up,
    value_up,
    block_order,
    tenant,
):
    my_index = lax.axis_index("ctx")
    x, z, core = my_index // 16, lax.rem(my_index // 2, ZS), lax.rem(my_index, 2)
    y = lax.axis_index("tp")
    block_id = lax.dynamic_index_in_dim(block_order, my_index, 0, keepdims=False)
    owner = lax.dynamic_index_in_dim(tenant, block_id, 0, keepdims=False)
    flags = [x % 2, x // 2, z % 2, (z // 2) % 2, z // 4]
    around = lax.rem(x - y + XS, XS)
    numbers = jnp.stack([around, block_id, core, x, owner] + flags).astype(jnp.int32)
    fx, bx = (lambda v: ctx_move(v, dx=1)), (lambda v: ctx_move(v, dx=-1))
    fz, bz = (lambda v: ctx_move(v, dz=1)), (lambda v: ctx_move(v, dz=-1))

    packed = query_rows.reshape(8, 4, 256).transpose(1, 0, 2).reshape(32, 256)
    blank = jnp.zeros((LINE_SENT - LINE, 256), BF)
    line = jnp.concatenate(
        [jnp.concatenate([key_weight, value_weight], axis=1), packed, swap_core(packed), blank], axis=0
    )
    line = gather_z(line[None])
    own, theirs = split_parity(core, hidden)
    own_1 = move_y(own, 1)
    other = swap_core(theirs)
    other_1 = move_y(other, -1)
    weight = jnp.stack([query_weight, fx(query_weight), ctx_move(query_weight, dx=2), bx(query_weight)])
    own_1, other_1, weight, hidden = tie(own_1, other_1, weight, hidden)
    own_2, other_2 = move_y(own_1, 1), move_y(other_1, -1)
    low = low_parts(numbers, hidden, query_down, value_down)
    own_2, other_2, line, weight, low = tie(own_2, other_2, line, weight, low)
    weight = gather_z(weight[None])
    line = line[:, :LINE]
    ahead, behind = fx(line), bx(line)
    own_3, other_3 = move_y(own_2, 1), move_y(other_2, -1)
    low = low + lax.ppermute(low, "tp", [(i, i ^ 1) for i in range(YS)])
    own_3, other_3, ahead, behind, low = tie(own_3, other_3, ahead, behind, low)
    far = jnp.concatenate([fx(ahead[:4]), bx(behind[4:])], axis=0)
    low = low + lax.ppermute(low, "tp", [(i, i ^ 2) for i in range(YS)])
    lines = jnp.stack([line, ahead, far, behind])
    own_tokens = (own, own_1, own_2, own_3)
    other_tokens = (other, other_1, other_2, other_3)

    low = low.astype(BF)
    over_rank = (((0,), (0,)), ((), ()))
    query_lift = lax.dot_general(
        low[:RANK], lax.dynamic_index_in_dim(query_up, owner, 0, keepdims=False), over_rank, preferred_element_type=F32
    )
    value_lift = lax.dot_general(
        low[RANK:], lax.dynamic_index_in_dim(value_up, owner, 0, keepdims=False), over_rank, preferred_element_type=F32
    )
    half = HEAD // 2
    positions = block_id * ROWS + jnp.arange(ROWS, dtype=jnp.int32)
    frequency = rope_base ** (-(jnp.arange(half, dtype=F32) / half))
    angles = positions.astype(F32)[:, None] * frequency[None, :]
    cosine, sine = jnp.cos(angles), jnp.sin(angles)
    cosine = jnp.concatenate([cosine, cosine], axis=1)
    sine = jnp.concatenate([-sine, sine], axis=1)

    own_part, part = project(numbers, own_tokens, other_tokens, lines)
    pair = finish_keys(own_part, swap_core(part), value_lift, cosine, sine)

    keep, send = query_attention(numbers, lines, pair)
    for bit, at, group in ((CORE, 0, 64), (X1, 1, 64), (X2, 2, 8)):
        keep, send = merge(numbers, keep, send, ctx_flip(send, bit), FLAGS + at, group)
    got, parts = tie(ctx_flip(send, Z1), project(numbers, own_tokens, other_tokens, weight))
    own_part, part = parts
    keep, send = merge(numbers, keep, send, got, FLAGS + 3, 8)
    got, got_part = tie(ctx_flip(send, Z2), swap_core(part))
    keep, send = merge(numbers, keep, send, got, FLAGS + 4, 8)
    answer, mine = merge(numbers, keep, send, ctx_flip(send, Z4))
    context = context_attention(
        numbers, own_part, got_part, query_lift, cosine, sine, pair, mine, swap_core(mine)
    )
    return (context, answer)


def solution(mesh):
    placed = (
        P("ctx", "tp"),
        P("ctx", "tp"),
        P("ctx", "tp"),
        P("ctx", "tp"),
        P("ctx", "tp"),
        P("tp", None),
        P("tp", None),
        P(None, None, "tp"),
        P(None, None, "tp"),
        P(),
        P(),
    )
    return jax.shard_map(
        shards,
        mesh=mesh,
        in_specs=placed,
        out_specs=(P("ctx", "tp"), P("ctx", "tp")),
        check_vma=False,
    )
```

```python
import functools

import jax
import jax.numpy as jnp
from jax import lax
from jax.experimental import pallas as pl
from jax.experimental.pallas import tpu as pltpu
from jax.sharding import PartitionSpec as P

HEAD = 128
RANK = 16
XS, ZS, YS = 4, 8, 4
CORE, Z1, Z2, Z4, X1, X2 = 1, 2, 4, 8, 16, 32
LINE_SENT = 256
LINE = 192
AROUND, BLOCK_ID, CORE_AT, PLACE_X, OWNER, FLAGS = 0, 1, 2, 3, 4, 5
ROWS = 448
VMEM = 32 * 1024 * 1024
BF = jnp.bfloat16
F32 = jnp.float32

rope_base = 500000.0
masked = -1e30
scale = HEAD ** (-0.5)
power = scale * 1.4426950408889634


def place(x, z, core):
    return (x % XS) * 16 + (z % ZS) * 2 + core


def ctx_move(value, dx=0, dz=0, swap=False):
    pairs = []
    for x in range(XS):
        for z in range(ZS):
            for core in range(2):
                pairs.append((place(x, z, core), place(x + dx, z + dz, 1 - core if swap else core)))
    return lax.ppermute(value, "ctx", pairs)


def ctx_flip(value, bit):
    return lax.ppermute(value, "ctx", [(i, i ^ bit) for i in range(64)])


def swap_core(value):
    return ctx_move(value, swap=True)


def gather_z(value):
    lines = [[place(x, z, core) for z in range(ZS)] for x in range(XS) for core in range(2)]
    return lax.all_gather(value, "ctx", axis_index_groups=lines, axis=0, tiled=True)


def move_y(value, dy):
    return lax.ppermute(value, "tp", [(y, (y + dy) % YS) for y in range(YS)])


def ring(piece, count, forward, backward):
    pieces = [None] * count
    pieces[0] = piece
    ahead = behind = piece
    for step in range(1, count // 2):
        ahead, behind = forward(ahead), backward(behind)
        pieces[step], pieces[count - step] = ahead, behind
    half = piece.shape[0] // 2
    pieces[count // 2] = (forward(ahead[:half]), backward(behind[half:]))
    return pieces


def ordered(pieces, me):
    count = len(pieces)
    buffer = jnp.zeros((count,) + pieces[0].shape, pieces[0].dtype)
    zeros = (0,) * (pieces[0].ndim - 1)
    for back, piece in enumerate(pieces):
        at = lax.rem(me - back + count, count)
        if isinstance(piece, tuple):
            low, high = piece
            buffer = lax.dynamic_update_slice(buffer, low[None], (at, 0) + zeros)
            buffer = lax.dynamic_update_slice(buffer, high[None], (at, low.shape[0]) + zeros)
        else:
            buffer = lax.dynamic_update_slice(buffer, piece[None], (at, 0) + zeros)
    return buffer


def call(kernel, flops, moved, exps=0, vmem=VMEM, **kw):
    return pl.pallas_call(
        kernel,
        compiler_params=pltpu.CompilerParams(vmem_limit_bytes=vmem),
        cost_estimate=pl.CostEstimate(flops=flops, bytes_accessed=moved, transcendentals=exps),
        **kw,
    )


def pack_terms(values, step):
    high = values.astype(BF).astype(F32)
    rest = values - high
    middle = rest.astype(BF).astype(F32)
    low = rest - middle
    return high + pltpu.roll(middle, step, 1) + pltpu.roll(low, 2 * step, 1)


def unpack_terms(group, step):
    terms = group.astype(F32)
    return terms + pltpu.roll(terms, 128 - step, 1) + pltpu.roll(terms, 128 - 2 * step, 1)


def theirs_kernel(core_ref, hidden_ref, out_ref):
    for block in range(8):
        even = hidden_ref[:, block * 256 : block * 256 + 128]
        odd = hidden_ref[:, block * 256 + 128 : block * 256 + 256]
        out_ref[:, block * 128 : block * 128 + 128] = jnp.where(core_ref[0] == 0, odd, even)


def theirs_of(core, hidden):
    vmem = pl.BlockSpec(memory_space=pltpu.VMEM)
    return call(
        theirs_kernel,
        0,
        3 * ROWS * 2048,
        out_shape=jax.ShapeDtypeStruct((ROWS, 1024), BF),
        in_specs=[pl.BlockSpec(memory_space=pltpu.SMEM), vmem],
        out_specs=vmem,
    )(core.reshape(1), hidden)


def own_kernel(number_ref, hidden_ref, query_ref, value_ref, out_ref):
    shift = number_ref[OWNER] * RANK
    low_q = jnp.dot(hidden_ref[...], query_ref[...], preferred_element_type=F32)
    low_v = jnp.dot(hidden_ref[...], value_ref[...], preferred_element_type=F32)
    low_q = pltpu.roll(low_q, lax.rem(128 - shift, 128), 1)
    low_v = pltpu.roll(low_v, lax.rem(128 + RANK - shift, 128), 1)
    lane = lax.broadcasted_iota(jnp.int32, low_q.shape, 1)
    low = jnp.where(lane < RANK, low_q, jnp.where(lane < 2 * RANK, low_v, 0.0))
    out_ref[:, 1024:] = pack_terms(low, 2 * RANK).astype(BF)
    first = number_ref[CORE_AT] == 0
    for block in range(8):
        even = hidden_ref[:, block * 256 : block * 256 + 128]
        odd = hidden_ref[:, block * 256 + 128 : block * 256 + 256]
        out_ref[:, block * 128 : block * 128 + 128] = jnp.where(first, even, odd)


def own_of(numbers, hidden, query_down, value_down):
    vmem = pl.BlockSpec(memory_space=pltpu.VMEM)
    return call(
        own_kernel,
        2 * ROWS * 2048 * 256,
        3 * ROWS * 2048 + 2 * 2048 * 256,
        out_shape=jax.ShapeDtypeStruct((ROWS, 1152), BF),
        in_specs=[pl.BlockSpec(memory_space=pltpu.SMEM)] + [vmem] * 3,
        out_specs=vmem,
    )(numbers, hidden, query_down, value_down)


def project_kernel(number_ref, *refs):
    own_refs, other_refs, weight_ref, own_out, other_out = refs[:4], refs[4:8], refs[8], refs[9], refs[10]
    if len(refs) == 12:
        low = sum(unpack_terms(ref[:, 1024:], 2 * RANK) for ref in own_refs)
        lane = lax.broadcasted_iota(jnp.int32, low.shape, 1)
        refs[11][...] = jnp.where(lane < 2 * RANK, low, 0.0).astype(BF)
    sums = None
    for step in range(YS):
        at = lax.rem(number_ref[AROUND] + step, YS)
        if weight_ref.shape[0] == XS:
            blocks = [weight_ref[at, block, :128] for block in range(ZS)]
        else:
            blocks = [weight_ref[block, at] for block in range(ZS)]
        tokens = jnp.concatenate([own_refs[step][:, :1024], other_refs[step][...]], axis=0)
        product = jnp.dot(tokens, jnp.concatenate(blocks, axis=0), preferred_element_type=F32)
        sums = product if sums is None else sums + product
    own_out[...] = sums[:ROWS]
    other_out[...] = sums[ROWS:]


def project(numbers, tokens, weight, at=0, cols=256):
    out = jax.ShapeDtypeStruct((ROWS, cols), F32)
    vmem = pl.BlockSpec(memory_space=pltpu.VMEM)
    tile = pl.BlockSpec((ROWS, 256), lambda i: (0, i))
    window = None
    if cols > 256:
        window = pl.BlockSpec(weight.shape[:-1] + (256,), lambda i: (0, 0, 0, i + at))
    return call(
        project_kernel,
        4 * ROWS * 4096 * cols,
        2 * 4096 * (2 * ROWS + cols) + 8 * ROWS * cols,
        vmem=VMEM if cols == 256 else 50 * 1024 * 1024,
        out_shape=(out, out) + ((jax.ShapeDtypeStruct((ROWS, 128), BF),) if cols == 256 else ()),
        grid=(cols // 256,),
        in_specs=[pl.BlockSpec(memory_space=pltpu.SMEM)] + [vmem] * 8 + [vmem if cols == 256 else window],
        out_specs=(tile, tile) + ((pl.BlockSpec((ROWS, 128), lambda i: (0, 0)),) if cols == 256 else ()),
    )(numbers, *tokens, weight)


def turn(values, cosine, sine):
    return values * cosine + pltpu.roll(values, HEAD // 2, 1) * sine


def against(queries, keys):
    return lax.dot_general(queries, keys, (((1,), (1,)), ((), ())), preferred_element_type=F32)


def attend(queries, first, pair_ref, anchor_ref):
    to_anchor = against(queries, anchor_ref[:, :HEAD])
    to_anchor = jnp.where(first, masked, to_anchor)
    to_own = against(queries, pair_ref[:, :HEAD])
    row = lax.broadcasted_iota(jnp.int32, (ROWS, ROWS), 0)
    col = lax.broadcasted_iota(jnp.int32, (ROWS, ROWS), 1)
    to_own = jnp.where(row >= col, to_own, masked)
    highest = jnp.maximum(
        jnp.max(to_anchor, axis=1, keepdims=True), jnp.max(to_own, axis=1, keepdims=True)
    )
    to_anchor = jnp.exp2((to_anchor - highest) * power)
    to_own = jnp.exp2((to_own - highest) * power)
    total = jnp.sum(to_anchor, axis=1, keepdims=True) + jnp.sum(to_own, axis=1, keepdims=True)
    share = 1.0 / total
    mixed = jnp.dot((to_anchor * share).astype(BF), anchor_ref[:, HEAD:], preferred_element_type=F32)
    return mixed + jnp.dot((to_own * share).astype(BF), pair_ref[:, HEAD:], preferred_element_type=F32)


def unpacked(group_ref):
    return jnp.concatenate([group_ref[:, g * HEAD : (g + 1) * HEAD] for g in range(7)], axis=0)


def context_kernel(
    number_ref,
    own_ref,
    got_ref,
    own_late_ref,
    got_late_ref,
    low_ref,
    up_ref,
    cos_ref,
    sin_ref,
    pair_ref,
    mine_ref,
    theirs_ref,
    out_ref,
    anchor_ref,
):
    step = pl.program_id(0)

    @pl.when(step == 0)
    def _():
        mine, theirs = unpacked(mine_ref), unpacked(theirs_ref)
        anchor_ref[:, :HEAD] = jnp.where(number_ref[CORE_AT] == 0, mine, theirs)
        anchor_ref[:, HEAD:] = jnp.where(number_ref[CORE_AT] == 0, theirs, mine)

    queries = jnp.where(step < 2, own_ref[...] + got_ref[...], own_late_ref[...] + got_late_ref[...])
    queries = queries + jnp.dot(low_ref[...], up_ref[...], preferred_element_type=F32)
    for head in range(2):
        cols = slice(head * HEAD, (head + 1) * HEAD)
        turned = turn(queries[:, cols], cos_ref[...], sin_ref[...]).astype(BF)
        out_ref[:, cols] = attend(turned, number_ref[BLOCK_ID] == 0, pair_ref, anchor_ref).astype(BF)


def context_attention(numbers, early, late, low, up, cosine, sine, pair, mine, theirs):
    wide = pl.BlockSpec((ROWS, 256), lambda i: (0, 0))
    thin = pl.BlockSpec((ROWS, 128), lambda i: (0, 0))
    heads = pl.BlockSpec((ROWS, 256), lambda i: (0, i))
    lifts = pl.BlockSpec((128, 256), lambda i: (0, i))
    first = pl.BlockSpec((ROWS, 256), lambda i: (0, jnp.minimum(i, 1)))
    last = pl.BlockSpec((ROWS, 256), lambda i: (0, jnp.maximum(i - 2, 0)))
    packed = pl.BlockSpec((64, 1152), lambda i: (0, 0))
    return call(
        context_kernel,
        64 * ROWS * ROWS * HEAD,
        ROWS * 1024 * 14,
        16 * ROWS * ROWS,
        out_shape=jax.ShapeDtypeStruct((ROWS, 1024), BF),
        grid=(4,),
        in_specs=[pl.BlockSpec(memory_space=pltpu.SMEM)]
        + [first, first, last, last, thin, lifts, thin, thin, wide, packed, packed],
        out_specs=heads,
        scratch_shapes=[pltpu.VMEM((ROWS, 256), BF)],
    )(numbers, *early, *late, low, up, cosine, sine, pair, mine, theirs)


def stats_of(maxima, totals):
    rows = maxima[0].shape[0]
    lane = lax.broadcasted_iota(jnp.int32, (rows, 128), 1)
    stats = jnp.zeros((rows, 128), F32)
    for at, column in enumerate(maxima + totals):
        stats = jnp.where(lane == at, column, stats)
    return stats


def put(keep_ref, send_ref, top, cols, value, group, flag, stats=False):
    half = value.shape[0] // 2
    split = value.reshape(half // group, 2, group, value.shape[1])
    low, high = split[:, 0].reshape(half, -1), split[:, 1].reshape(half, -1)
    keep_ref[:, cols] = jnp.where(flag, high, low)
    sent = jnp.where(flag, low, high)
    if stats:
        sent = pack_terms(sent, 16)
    if half < 16:
        sent = jnp.concatenate([sent, sent], axis=0)
    send_ref[top:, cols] = sent.astype(BF)


def query_kernel(
    number_ref,
    lines_ref,
    own_ref,
    got_ref,
    low_ref,
    up_ref,
    cos_ref,
    sin_ref,
    keep_ref,
    send_ref,
    pair_ref,
    query_ref,
):
    lift = jnp.dot(low_ref[...], up_ref[...], preferred_element_type=F32)
    keys = own_ref[:, :HEAD] + got_ref[:, :HEAD]
    pair_ref[:, :HEAD] = turn(keys, cos_ref[...], sin_ref[...]).astype(BF)
    pair_ref[:, HEAD:] = (own_ref[:, HEAD:] + got_ref[:, HEAD:] + lift).astype(BF)

    for side in range(2):
        for at_x in range(XS):
            back = lax.rem(number_ref[PLACE_X] + XS - at_x, XS)
            for pair in range(4):
                rows = []
                for place in (2 * pair, 2 * pair + 1):
                    block = lines_ref[back, place, 128 + 32 * side : 160 + 32 * side].astype(F32)
                    rows.append(jnp.concatenate([block[8 * g : 8 * g + 8] for g in range(4)], axis=1))
                at = 256 * side + 64 * at_x + 16 * pair
                query_ref[at : at + 16] = jnp.concatenate(rows, axis=0).astype(BF)

    send_ref[:128, 896:] = jnp.zeros((128, 256), BF)
    for half in range(2):
        cols = slice(half * HEAD, (half + 1) * HEAD)
        for g in range(7):
            piece = pair_ref[g * 64 : g * 64 + 64, cols]
            send_ref[half * 64 : half * 64 + 64, g * HEAD : (g + 1) * HEAD] = jnp.where(
                number_ref[BLOCK_ID] == 0, piece, jnp.zeros_like(piece)
            )
    rows = query_ref.shape[0]
    maxima, totals = [], []
    for head in range(8):
        cols = slice(head * HEAD, (head + 1) * HEAD)
        scores = against(query_ref[:, cols], pair_ref[:, :HEAD])
        highest = jnp.max(scores, axis=1, keepdims=True)
        weights = jnp.exp2((scores - highest) * power)
        maxima.append(highest * scale)
        totals.append(jnp.sum(weights, axis=1, keepdims=True))
        sums = jnp.dot(weights.astype(BF), pair_ref[:, HEAD:], preferred_element_type=F32)
        put(keep_ref, send_ref, 128, cols, sums, rows // 2, False)
    put(keep_ref, send_ref, 128, slice(1024, 1152), stats_of(maxima, totals), rows // 2, False, True)


def merge_kernel(group, at_flag, number_ref, mine_ref, sent_ref, got_ref, *out):
    flag = number_ref[at_flag] == 1
    rows = mine_ref.shape[0]
    top = 64 if rows < 256 else 128
    anchor = sent_ref[:top] + got_ref[:top]
    if top == 128:
        anchor = jnp.where(number_ref[CORE_AT] == 0, anchor[:64], anchor[64:])
    out[1][:64] = anchor
    lane = lax.broadcasted_iota(jnp.int32, (rows, 128), 1)
    one, two = mine_ref[:, 1024:], unpack_terms(got_ref[top:, 1024:], 16)[:rows]
    highest = jnp.maximum(one, two)
    left = jnp.exp(jnp.where(lane < 8, one - highest, 0.0))
    right = jnp.exp(jnp.where(lane < 8, two - highest, 0.0))
    totals = one * pltpu.roll(left, 8, 1) + two * pltpu.roll(right, 8, 1)
    for head in range(8):
        cols = slice(head * HEAD, (head + 1) * HEAD)
        at = slice(head, head + 1)
        other = got_ref[top:, cols].astype(F32)[:rows]
        merged = mine_ref[:, cols] * left[:, at] + other * right[:, at]
        if group is None:
            out[0][:, cols] = (merged / totals[:, head + 8 : head + 9]).astype(BF)
        else:
            put(out[0], out[1], 64, cols, merged, group, flag)
    if group is not None:
        stats = jnp.where(lane < 8, highest, jnp.where(lane < 16, totals, 0.0))
        put(out[0], out[1], 64, slice(1024, 1152), stats, group, flag, True)


VMEM_BLOCK = pl.BlockSpec(memory_space=pltpu.VMEM)


def query_attention(numbers, lines, own, got, low, up, cosine, sine):
    rows = 512
    return call(
        query_kernel,
        32 * rows * ROWS * HEAD,
        rows * 1024 * 6,
        8 * rows * ROWS,
        out_shape=(
            jax.ShapeDtypeStruct((rows // 2, 1152), F32),
            jax.ShapeDtypeStruct((128 + rows // 2, 1152), BF),
            jax.ShapeDtypeStruct((ROWS, 256), BF),
        ),
        in_specs=[pl.BlockSpec(memory_space=pltpu.SMEM)] + [VMEM_BLOCK] * 7,
        out_specs=(VMEM_BLOCK,) * 3,
        scratch_shapes=[pltpu.VMEM((rows, 1024), BF)],
    )(numbers, lines, own, got, low, up, cosine, sine)


def merge(numbers, mine, sent, got, at_flag=0, group=None):
    rows = mine.shape[0]
    if group is None:
        shapes = (jax.ShapeDtypeStruct((rows, 1024), BF), jax.ShapeDtypeStruct((64, 1152), BF))
    else:
        half = rows // 2
        shapes = (
            jax.ShapeDtypeStruct((half, 1152), F32),
            jax.ShapeDtypeStruct((64 + max(half, 16), 1152), BF),
        )
    return call(
        functools.partial(merge_kernel, group, at_flag),
        8 * rows * 1024,
        rows * 1152 * 8,
        out_shape=shapes,
        in_specs=[pl.BlockSpec(memory_space=pltpu.SMEM)] + [VMEM_BLOCK] * 3,
        out_specs=(VMEM_BLOCK,) * 2,
    )(numbers, mine, sent, got)


def tie(*values):
    return lax.optimization_barrier(values)


def doubled(piece, bit_set, got):
    return jnp.concatenate([jnp.where(bit_set, got, piece), jnp.where(bit_set, piece, got)], axis=0)


def shards(
    hidden,
    query_rows,
    query_weight,
    key_weight,
    value_weight,
    query_down,
    value_down,
    query_up,
    value_up,
    block_order,
    tenant,
):
    my_index = lax.axis_index("ctx")
    x, z, core = my_index // 16, lax.rem(my_index // 2, ZS), lax.rem(my_index, 2)
    y = lax.axis_index("tp")
    block_id = lax.dynamic_index_in_dim(block_order, my_index, 0, keepdims=False)
    owner = lax.dynamic_index_in_dim(tenant, block_id, 0, keepdims=False)
    flags = [x % 2, x // 2, z % 2, (z // 2) % 2, z // 4]
    around = lax.rem(x - y + XS, XS)
    numbers = jnp.stack([around, block_id, core, x, owner] + flags).astype(jnp.int32)
    fx, bx = (lambda v: ctx_move(v, dx=1)), (lambda v: ctx_move(v, dx=-1))
    fz, bz = (lambda v: ctx_move(v, dz=1)), (lambda v: ctx_move(v, dz=-1))

    packed = query_rows.reshape(8, 4, 256).transpose(1, 0, 2).reshape(32, 256)
    blank = jnp.zeros((LINE_SENT - LINE, 256), BF)
    line = jnp.concatenate(
        [jnp.concatenate([key_weight, value_weight], axis=1), packed, swap_core(packed), blank], axis=0
    )
    line = gather_z(line[None])
    other = swap_core(theirs_of(core, hidden))
    other_1, other_3 = move_y(other, 1), move_y(other, -1)
    weight = jnp.stack([query_weight, fx(query_weight), ctx_move(query_weight, dx=2), bx(query_weight)])
    own = own_of(numbers, hidden, query_down, value_down)
    other_1, other_3, weight, own = tie(other_1, other_3, weight, own)
    own_1, own_3 = move_y(own, 1), move_y(own, -1)
    line, weight = tie(line, weight)
    weight = gather_z(weight[None])
    line = line[:, :LINE]
    ahead, behind = fx(line), bx(line)
    own_1, own_3, other_3, ahead, behind = tie(own_1, own_3, other_3, ahead, behind)
    own_2, other_2 = move_y(own_1, 1), move_y(other_3, -1)
    far = (fx(ahead[:4]), bx(behind[4:]))

    tokens = (own, own_1, own_2, own_3, other, other_1, other_2, other_3)

    query_up = lax.dynamic_index_in_dim(query_up, owner, 0, keepdims=False)
    value_up = lax.dynamic_index_in_dim(value_up, owner, 0, keepdims=False)
    query_up = jnp.pad(query_up, ((0, 128 - RANK), (0, 0)))
    value_up = jnp.pad(value_up, ((RANK, 128 - 2 * RANK), (0, 0)))
    half = HEAD // 2
    positions = block_id * ROWS + jnp.arange(ROWS, dtype=jnp.int32)
    frequency = rope_base ** (-(jnp.arange(half, dtype=F32) / half))
    angles = positions.astype(F32)[:, None] * frequency[None, :]
    cosine, sine = jnp.cos(angles), jnp.sin(angles)
    cosine = jnp.concatenate([cosine, cosine], axis=1)
    sine = jnp.concatenate([-sine, sine], axis=1)

    far, cosine, sine, value_up = tie(far, cosine, sine, value_up)
    lines = jnp.stack([line, ahead, jnp.concatenate(far, axis=0), behind])
    own_part, part, low = project(numbers, tokens, lines)
    keep, send, pair = query_attention(numbers, lines, own_part, swap_core(part), low, value_up, cosine, sine)
    for bit, at, group in ((CORE, 0, 64), (X1, 1, 64), (X2, 2, 8), (Z1, 3, 8)):
        keep, send = merge(numbers, keep, send, ctx_flip(send, bit), FLAGS + at, group)
    got, parts = tie(ctx_flip(send, Z2), project(numbers, tokens, weight, 0, 512))
    own_early, part = parts
    keep, send = merge(numbers, keep, send, got, FLAGS + 4, 8)
    got, got_early, parts = tie(ctx_flip(send, Z4), swap_core(part), project(numbers, tokens, weight, 2, 512))
    own_late, part = parts
    got_late = swap_core(part)
    answer, mine = merge(numbers, keep, send, got)
    context = context_attention(
        numbers,
        (own_early, got_early),
        (own_late, got_late),
        low,
        query_up,
        cosine,
        sine,
        pair,
        mine,
        swap_core(mine),
    )
    return (context, answer)


def solution(mesh):
    placed = (
        P("ctx", "tp"),
        P("ctx", "tp"),
        P("ctx", "tp"),
        P("ctx", "tp"),
        P("ctx", "tp"),
        P("tp", None),
        P("tp", None),
        P(None, None, "tp"),
        P(None, None, "tp"),
        P(),
        P(),
    )
    return jax.shard_map(
        shards,
        mesh=mesh,
        in_specs=placed,
        out_specs=(P("ctx", "tp"), P("ctx", "tp")),
        check_vma=False,
    )
```

```python
import functools

import jax
import jax.numpy as jnp
from jax import lax
from jax.experimental import pallas as pl
from jax.experimental.pallas import tpu as pltpu
from jax.sharding import PartitionSpec as P

HEAD = 128
RANK = 16
XS, ZS, YS = 4, 8, 4
CORE, Z1, Z2, Z4, X1, X2 = 1, 2, 4, 8, 16, 32
LINE_SENT = 256
LINE = 160
AROUND, BLOCK_ID, CORE_AT, PLACE_X, OWNER, FLAGS = 0, 1, 2, 3, 4, 5
ROWS = 448
VMEM = 32 * 1024 * 1024
BF = jnp.bfloat16
F32 = jnp.float32

rope_base = 500000.0
masked = -1e30
scale = HEAD ** (-0.5)
power = scale * 1.4426950408889634


def place(x, z, core):
    return (x % XS) * 16 + (z % ZS) * 2 + core


def ctx_move(value, dx=0, dz=0, swap=False):
    pairs = []
    for x in range(XS):
        for z in range(ZS):
            for core in range(2):
                pairs.append((place(x, z, core), place(x + dx, z + dz, 1 - core if swap else core)))
    return lax.ppermute(value, "ctx", pairs)


def ctx_flip(value, bit):
    return lax.ppermute(value, "ctx", [(i, i ^ bit) for i in range(64)])


def swap_core(value):
    return ctx_move(value, swap=True)


def gather_z(value):
    lines = [[place(x, z, core) for z in range(ZS)] for x in range(XS) for core in range(2)]
    return lax.all_gather(value, "ctx", axis_index_groups=lines, axis=0, tiled=True)


def move_y(value, dy):
    return lax.ppermute(value, "tp", [(y, (y + dy) % YS) for y in range(YS)])


def ring(piece, count, forward, backward):
    pieces = [None] * count
    pieces[0] = piece
    ahead = behind = piece
    for step in range(1, count // 2):
        ahead, behind = forward(ahead), backward(behind)
        pieces[step], pieces[count - step] = ahead, behind
    half = piece.shape[0] // 2
    pieces[count // 2] = (forward(ahead[:half]), backward(behind[half:]))
    return pieces


def ordered(pieces, me):
    count = len(pieces)
    buffer = jnp.zeros((count,) + pieces[0].shape, pieces[0].dtype)
    zeros = (0,) * (pieces[0].ndim - 1)
    for back, piece in enumerate(pieces):
        at = lax.rem(me - back + count, count)
        if isinstance(piece, tuple):
            low, high = piece
            buffer = lax.dynamic_update_slice(buffer, low[None], (at, 0) + zeros)
            buffer = lax.dynamic_update_slice(buffer, high[None], (at, low.shape[0]) + zeros)
        else:
            buffer = lax.dynamic_update_slice(buffer, piece[None], (at, 0) + zeros)
    return buffer


def call(kernel, flops, moved, exps=0, vmem=VMEM, **kw):
    return pl.pallas_call(
        kernel,
        compiler_params=pltpu.CompilerParams(vmem_limit_bytes=vmem),
        cost_estimate=pl.CostEstimate(flops=flops, bytes_accessed=moved, transcendentals=exps),
        **kw,
    )


def pack_terms(values, step):
    high = values.astype(BF).astype(F32)
    rest = values - high
    middle = rest.astype(BF).astype(F32)
    low = rest - middle
    return high + pltpu.roll(middle, step, 1) + pltpu.roll(low, 2 * step, 1)


def unpack_terms(group, step):
    terms = group.astype(F32)
    return terms + pltpu.roll(terms, 128 - step, 1) + pltpu.roll(terms, 128 - 2 * step, 1)


def theirs_kernel(core_ref, hidden_ref, out_ref):
    for block in range(8):
        even = hidden_ref[:, block * 256 : block * 256 + 128]
        odd = hidden_ref[:, block * 256 + 128 : block * 256 + 256]
        out_ref[:, block * 128 : block * 128 + 128] = jnp.where(core_ref[0] == 0, odd, even)


def theirs_of(core, hidden):
    vmem = pl.BlockSpec(memory_space=pltpu.VMEM)
    return call(
        theirs_kernel,
        0,
        3 * ROWS * 2048,
        out_shape=jax.ShapeDtypeStruct((ROWS, 1024), BF),
        in_specs=[pl.BlockSpec(memory_space=pltpu.SMEM), vmem],
        out_specs=vmem,
    )(core.reshape(1), hidden)


def own_kernel(number_ref, hidden_ref, query_ref, value_ref, out_ref):
    shift = number_ref[OWNER] * RANK
    low_q = jnp.dot(hidden_ref[...], query_ref[...], preferred_element_type=F32)
    low_v = jnp.dot(hidden_ref[...], value_ref[...], preferred_element_type=F32)
    low_q = pltpu.roll(low_q, lax.rem(128 - shift, 128), 1)
    low_v = pltpu.roll(low_v, lax.rem(128 + RANK - shift, 128), 1)
    lane = lax.broadcasted_iota(jnp.int32, low_q.shape, 1)
    low = jnp.where(lane < RANK, low_q, jnp.where(lane < 2 * RANK, low_v, 0.0))
    out_ref[:, 1024:] = pack_terms(low, 2 * RANK).astype(BF)
    first = number_ref[CORE_AT] == 0
    for block in range(8):
        even = hidden_ref[:, block * 256 : block * 256 + 128]
        odd = hidden_ref[:, block * 256 + 128 : block * 256 + 256]
        out_ref[:, block * 128 : block * 128 + 128] = jnp.where(first, even, odd)


def own_of(numbers, hidden, query_down, value_down):
    vmem = pl.BlockSpec(memory_space=pltpu.VMEM)
    return call(
        own_kernel,
        2 * ROWS * 2048 * 256,
        3 * ROWS * 2048 + 2 * 2048 * 256,
        out_shape=jax.ShapeDtypeStruct((ROWS, 1152), BF),
        in_specs=[pl.BlockSpec(memory_space=pltpu.SMEM)] + [vmem] * 3,
        out_specs=vmem,
    )(numbers, hidden, query_down, value_down)


def project_kernel(number_ref, *refs):
    own_refs, other_refs, weight_ref, own_out, other_out = refs[:4], refs[4:8], refs[8], refs[9], refs[10]
    if len(refs) == 12:
        low = sum(unpack_terms(ref[:, 1024:], 2 * RANK) for ref in own_refs)
        lane = lax.broadcasted_iota(jnp.int32, low.shape, 1)
        refs[11][...] = jnp.where(lane < 2 * RANK, low, 0.0).astype(BF)
    sums = None
    for step in range(YS):
        at = lax.rem(number_ref[AROUND] + step, YS)
        if weight_ref.shape[0] == XS:
            blocks = [weight_ref[at, block, :128] for block in range(ZS)]
        else:
            blocks = [weight_ref[block, at] for block in range(ZS)]
        tokens = jnp.concatenate([own_refs[step][:, :1024], other_refs[step][...]], axis=0)
        product = jnp.dot(tokens, jnp.concatenate(blocks, axis=0), preferred_element_type=F32)
        sums = product if sums is None else sums + product
    own_out[...] = sums[:ROWS]
    other_out[...] = sums[ROWS:]


def project(numbers, tokens, weight, at=0, cols=256):
    out = jax.ShapeDtypeStruct((ROWS, cols), F32)
    vmem = pl.BlockSpec(memory_space=pltpu.VMEM)
    tile = pl.BlockSpec((ROWS, 256), lambda i: (0, i))
    window = None
    if cols > 256:
        window = pl.BlockSpec(weight.shape[:-1] + (256,), lambda i: (0, 0, 0, i + at))
    return call(
        project_kernel,
        4 * ROWS * 4096 * cols,
        2 * 4096 * (2 * ROWS + cols) + 8 * ROWS * cols,
        vmem=VMEM if cols == 256 else 50 * 1024 * 1024,
        out_shape=(out, out) + ((jax.ShapeDtypeStruct((ROWS, 128), BF),) if cols == 256 else ()),
        grid=(cols // 256,),
        in_specs=[pl.BlockSpec(memory_space=pltpu.SMEM)] + [vmem] * 8 + [vmem if cols == 256 else window],
        out_specs=(tile, tile) + ((pl.BlockSpec((ROWS, 128), lambda i: (0, 0)),) if cols == 256 else ()),
    )(numbers, *tokens, weight)


def turn(values, cosine, sine):
    return values * cosine + pltpu.roll(values, HEAD // 2, 1) * sine


def against(queries, keys):
    return lax.dot_general(queries, keys, (((1,), (1,)), ((), ())), preferred_element_type=F32)


def attend(queries, first, pair_ref, anchor_ref):
    to_anchor = against(queries, anchor_ref[:, :HEAD])
    to_anchor = jnp.where(first, masked, to_anchor)
    to_own = against(queries, pair_ref[:, :HEAD])
    row = lax.broadcasted_iota(jnp.int32, (ROWS, ROWS), 0)
    col = lax.broadcasted_iota(jnp.int32, (ROWS, ROWS), 1)
    to_own = jnp.where(row >= col, to_own, masked)
    highest = jnp.maximum(
        jnp.max(to_anchor, axis=1, keepdims=True), jnp.max(to_own, axis=1, keepdims=True)
    )
    to_anchor = jnp.exp2((to_anchor - highest) * power)
    to_own = jnp.exp2((to_own - highest) * power)
    total = jnp.sum(to_anchor, axis=1, keepdims=True) + jnp.sum(to_own, axis=1, keepdims=True)
    share = 1.0 / total
    mixed = jnp.dot((to_anchor * share).astype(BF), anchor_ref[:, HEAD:], preferred_element_type=F32)
    return mixed + jnp.dot((to_own * share).astype(BF), pair_ref[:, HEAD:], preferred_element_type=F32)


def unpacked(group_ref):
    return jnp.concatenate([group_ref[:, g * HEAD : (g + 1) * HEAD] for g in range(7)], axis=0)


def context_kernel(
    number_ref,
    own_ref,
    got_ref,
    own_late_ref,
    got_late_ref,
    low_ref,
    up_ref,
    cos_ref,
    sin_ref,
    pair_ref,
    mine_ref,
    theirs_ref,
    out_ref,
    anchor_ref,
):
    step = pl.program_id(0)

    @pl.when(step == 0)
    def _():
        mine, theirs = unpacked(mine_ref), unpacked(theirs_ref)
        anchor_ref[:, :HEAD] = jnp.where(number_ref[CORE_AT] == 0, mine, theirs)
        anchor_ref[:, HEAD:] = jnp.where(number_ref[CORE_AT] == 0, theirs, mine)

    queries = jnp.where(step < 2, own_ref[...] + got_ref[...], own_late_ref[...] + got_late_ref[...])
    queries = queries + jnp.dot(low_ref[...], up_ref[...], preferred_element_type=F32)
    for head in range(2):
        cols = slice(head * HEAD, (head + 1) * HEAD)
        turned = turn(queries[:, cols], cos_ref[...], sin_ref[...]).astype(BF)
        out_ref[:, cols] = attend(turned, number_ref[BLOCK_ID] == 0, pair_ref, anchor_ref).astype(BF)


def context_attention(numbers, early, late, low, up, cosine, sine, pair, mine, theirs):
    wide = pl.BlockSpec((ROWS, 256), lambda i: (0, 0))
    thin = pl.BlockSpec((ROWS, 128), lambda i: (0, 0))
    heads = pl.BlockSpec((ROWS, 256), lambda i: (0, i))
    lifts = pl.BlockSpec((128, 256), lambda i: (0, i))
    first = pl.BlockSpec((ROWS, 256), lambda i: (0, jnp.minimum(i, 1)))
    last = pl.BlockSpec((ROWS, 256), lambda i: (0, jnp.maximum(i - 2, 0)))
    packed = pl.BlockSpec((64, 1152), lambda i: (0, 0))
    return call(
        context_kernel,
        64 * ROWS * ROWS * HEAD,
        ROWS * 1024 * 14,
        16 * ROWS * ROWS,
        out_shape=jax.ShapeDtypeStruct((ROWS, 1024), BF),
        grid=(4,),
        in_specs=[pl.BlockSpec(memory_space=pltpu.SMEM)]
        + [first, first, last, last, thin, lifts, thin, thin, wide, packed, packed],
        out_specs=heads,
        scratch_shapes=[pltpu.VMEM((ROWS, 256), BF)],
    )(numbers, *early, *late, low, up, cosine, sine, pair, mine, theirs)


def stats_of(maxima, totals):
    rows = maxima[0].shape[0]
    lane = lax.broadcasted_iota(jnp.int32, (rows, 128), 1)
    stats = jnp.zeros((rows, 128), F32)
    for at, column in enumerate(maxima + totals):
        stats = jnp.where(lane == at, column, stats)
    return stats


def put(keep_ref, send_ref, top, cols, value, group, flag, stats=False):
    half = value.shape[0] // 2
    split = value.reshape(half // group, 2, group, value.shape[1])
    low, high = split[:, 0].reshape(half, -1), split[:, 1].reshape(half, -1)
    keep_ref[:, cols] = jnp.where(flag, high, low)
    sent = jnp.where(flag, low, high)
    if stats:
        sent = pack_terms(sent, 16)
    if half < 16:
        sent = jnp.concatenate([sent, sent], axis=0)
    send_ref[top:, cols] = sent.astype(BF)


def query_kernel(
    number_ref,
    lines_ref,
    rows_ref,
    own_ref,
    got_ref,
    low_ref,
    up_ref,
    cos_ref,
    sin_ref,
    keep_ref,
    send_ref,
    pair_ref,
    query_ref,
):
    lift = jnp.dot(low_ref[...], up_ref[...], preferred_element_type=F32)
    keys = own_ref[:, :HEAD] + got_ref[:, :HEAD]
    pair_ref[:, :HEAD] = turn(keys, cos_ref[...], sin_ref[...]).astype(BF)
    pair_ref[:, HEAD:] = (own_ref[:, HEAD:] + got_ref[:, HEAD:] + lift).astype(BF)

    for side in range(2):
        for at_x in range(XS):
            back = lax.rem(number_ref[PLACE_X] + XS - at_x, XS)
            for pair in range(4):
                rows = []
                for place in (2 * pair, 2 * pair + 1):
                    block = rows_ref[back, place] if side else lines_ref[back, place, 128:]
                    block = block.astype(F32)
                    rows.append(jnp.concatenate([block[8 * g : 8 * g + 8] for g in range(4)], axis=1))
                at = 256 * side + 64 * at_x + 16 * pair
                query_ref[at : at + 16] = jnp.concatenate(rows, axis=0).astype(BF)

    send_ref[:128, 896:] = jnp.zeros((128, 256), BF)
    for half in range(2):
        cols = slice(half * HEAD, (half + 1) * HEAD)
        for g in range(7):
            piece = pair_ref[g * 64 : g * 64 + 64, cols]
            send_ref[half * 64 : half * 64 + 64, g * HEAD : (g + 1) * HEAD] = jnp.where(
                number_ref[BLOCK_ID] == 0, piece, jnp.zeros_like(piece)
            )
    rows = query_ref.shape[0]
    maxima, totals = [], []
    for head in range(8):
        cols = slice(head * HEAD, (head + 1) * HEAD)
        scores = against(query_ref[:, cols], pair_ref[:, :HEAD])
        highest = jnp.max(scores, axis=1, keepdims=True)
        weights = jnp.exp2((scores - highest) * power)
        maxima.append(highest * scale)
        totals.append(jnp.sum(weights, axis=1, keepdims=True))
        sums = jnp.dot(weights.astype(BF), pair_ref[:, HEAD:], preferred_element_type=F32)
        put(keep_ref, send_ref, 128, cols, sums, rows // 2, False)
    put(keep_ref, send_ref, 128, slice(1024, 1152), stats_of(maxima, totals), rows // 2, False, True)


def merge_kernel(group, at_flag, number_ref, mine_ref, sent_ref, got_ref, *out):
    flag = number_ref[at_flag] == 1
    rows = mine_ref.shape[0]
    top = 64 if rows < 256 else 128
    anchor = sent_ref[:top] + got_ref[:top]
    if top == 128:
        anchor = jnp.where(number_ref[CORE_AT] == 0, anchor[:64], anchor[64:])
    if group is not None:
        out[1][:64] = anchor
    lane = lax.broadcasted_iota(jnp.int32, (rows, 128), 1)
    one, two = mine_ref[:, 1024:], unpack_terms(got_ref[top:, 1024:], 16)[:rows]
    highest = jnp.maximum(one, two)
    left = jnp.exp(jnp.where(lane < 8, one - highest, 0.0))
    right = jnp.exp(jnp.where(lane < 8, two - highest, 0.0))
    totals = one * pltpu.roll(left, 8, 1) + two * pltpu.roll(right, 8, 1)
    for head in range(8):
        cols = slice(head * HEAD, (head + 1) * HEAD)
        at = slice(head, head + 1)
        other = got_ref[top:, cols].astype(F32)[:rows]
        merged = mine_ref[:, cols] * left[:, at] + other * right[:, at]
        if group is None:
            out[0][:, cols] = (merged / totals[:, head + 8 : head + 9]).astype(BF)
        else:
            put(out[0], out[1], 64, cols, merged, group, flag)
    if group is not None:
        stats = jnp.where(lane < 8, highest, jnp.where(lane < 16, totals, 0.0))
        put(out[0], out[1], 64, slice(1024, 1152), stats, group, flag, True)


VMEM_BLOCK = pl.BlockSpec(memory_space=pltpu.VMEM)


def query_attention(numbers, lines, rows_got, own, got, low, up, cosine, sine):
    rows = 512
    return call(
        query_kernel,
        32 * rows * ROWS * HEAD,
        rows * 1024 * 6,
        8 * rows * ROWS,
        out_shape=(
            jax.ShapeDtypeStruct((rows // 2, 1152), F32),
            jax.ShapeDtypeStruct((128 + rows // 2, 1152), BF),
            jax.ShapeDtypeStruct((ROWS, 256), BF),
        ),
        in_specs=[pl.BlockSpec(memory_space=pltpu.SMEM)] + [VMEM_BLOCK] * 8,
        out_specs=(VMEM_BLOCK,) * 3,
        scratch_shapes=[pltpu.VMEM((rows, 1024), BF)],
    )(numbers, lines, rows_got, own, got, low, up, cosine, sine)


def merge(numbers, mine, sent, got, at_flag=0, group=None):
    rows = mine.shape[0]
    if group is None:
        shapes = (jax.ShapeDtypeStruct((rows, 1024), BF),)
    else:
        half = rows // 2
        shapes = (
            jax.ShapeDtypeStruct((half, 1152), F32),
            jax.ShapeDtypeStruct((64 + max(half, 16), 1152), BF),
        )
    return call(
        functools.partial(merge_kernel, group, at_flag),
        8 * rows * 1024,
        rows * 1152 * 8,
        out_shape=shapes,
        in_specs=[pl.BlockSpec(memory_space=pltpu.SMEM)] + [VMEM_BLOCK] * 3,
        out_specs=(VMEM_BLOCK,) * len(shapes),
    )(numbers, mine, sent, got)


def tie(*values):
    return lax.optimization_barrier(values)


def doubled(piece, bit_set, got):
    return jnp.concatenate([jnp.where(bit_set, got, piece), jnp.where(bit_set, piece, got)], axis=0)


def shards(
    hidden,
    query_rows,
    query_weight,
    key_weight,
    value_weight,
    query_down,
    value_down,
    query_up,
    value_up,
    block_order,
    tenant,
):
    my_index = lax.axis_index("ctx")
    x, z, core = my_index // 16, lax.rem(my_index // 2, ZS), lax.rem(my_index, 2)
    y = lax.axis_index("tp")
    block_id = lax.dynamic_index_in_dim(block_order, my_index, 0, keepdims=False)
    owner = lax.dynamic_index_in_dim(tenant, block_id, 0, keepdims=False)
    flags = [x % 2, x // 2, z % 2, (z // 2) % 2, z // 4]
    around = lax.rem(x - y + XS, XS)
    numbers = jnp.stack([around, block_id, core, x, owner] + flags).astype(jnp.int32)
    fx, bx = (lambda v: ctx_move(v, dx=1)), (lambda v: ctx_move(v, dx=-1))
    fz, bz = (lambda v: ctx_move(v, dz=1)), (lambda v: ctx_move(v, dz=-1))

    packed = query_rows.reshape(8, 4, 256).transpose(1, 0, 2).reshape(32, 256)
    blank = jnp.zeros((LINE_SENT - LINE, 256), BF)
    line = jnp.concatenate(
        [jnp.concatenate([key_weight, value_weight], axis=1), packed, blank], axis=0
    )
    line = gather_z(line[None])
    other = swap_core(theirs_of(core, hidden))
    other_1, other_3 = move_y(other, 1), move_y(other, -1)
    weight = jnp.stack([query_weight, fx(query_weight), ctx_move(query_weight, dx=2), bx(query_weight)])
    own = own_of(numbers, hidden, query_down, value_down)
    other_1, other_3, weight, own = tie(other_1, other_3, weight, own)
    own_1, own_3 = move_y(own, 1), move_y(own, -1)
    line, weight = tie(line, weight)
    weight = gather_z(weight[None])
    line = line[:, :LINE]
    ahead, behind = fx(line), bx(line)
    own_1, own_3, other_3, ahead, behind = tie(own_1, own_3, other_3, ahead, behind)
    own_2, other_2 = move_y(own_1, 1), move_y(other_3, -1)
    far = (fx(ahead[:4]), bx(behind[4:]))

    tokens = (own, own_1, own_2, own_3, other, other_1, other_2, other_3)

    query_up = lax.dynamic_index_in_dim(query_up, owner, 0, keepdims=False)
    value_up = lax.dynamic_index_in_dim(value_up, owner, 0, keepdims=False)
    query_up = jnp.pad(query_up, ((0, 128 - RANK), (0, 0)))
    value_up = jnp.pad(value_up, ((RANK, 128 - 2 * RANK), (0, 0)))
    half = HEAD // 2
    positions = block_id * ROWS + jnp.arange(ROWS, dtype=jnp.int32)
    frequency = rope_base ** (-(jnp.arange(half, dtype=F32) / half))
    angles = positions.astype(F32)[:, None] * frequency[None, :]
    cosine, sine = jnp.cos(angles), jnp.sin(angles)
    cosine = jnp.concatenate([cosine, cosine], axis=1)
    sine = jnp.concatenate([-sine, sine], axis=1)

    far, cosine, sine, value_up = tie(far, cosine, sine, value_up)
    lines = jnp.stack([line, ahead, jnp.concatenate(far, axis=0), behind])
    own_part, part, low = project(numbers, tokens, lines)
    keep, send, pair = query_attention(numbers, lines, swap_core(lines[:, :, 128:]), own_part, swap_core(part), low, value_up, cosine, sine)
    for bit, at, group in ((CORE, 0, 64), (X1, 1, 64), (X2, 2, 8), (Z1, 3, 8)):
        keep, send = merge(numbers, keep, send, ctx_flip(send, bit), FLAGS + at, group)
    got, parts = tie(ctx_flip(send, Z2), project(numbers, tokens, weight, 0, 512))
    own_early, part = parts
    keep, send = merge(numbers, keep, send, got, FLAGS + 4, 8)
    got, got_early, parts = tie(ctx_flip(send, Z4), swap_core(part), project(numbers, tokens, weight, 2, 512))
    own_late, part = parts
    got_late = swap_core(part)
    mine = send[:64] + got[:64]
    (answer,) = merge(numbers, keep, send, got)
    context = context_attention(
        numbers,
        (own_early, got_early),
        (own_late, got_late),
        low,
        query_up,
        cosine,
        sine,
        pair,
        mine,
        swap_core(mine),
    )
    return (context, answer)


def solution(mesh):
    placed = (
        P("ctx", "tp"),
        P("ctx", "tp"),
        P("ctx", "tp"),
        P("ctx", "tp"),
        P("ctx", "tp"),
        P("tp", None),
        P("tp", None),
        P(None, None, "tp"),
        P(None, None, "tp"),
        P(),
        P(),
    )
    return jax.shard_map(
        shards,
        mesh=mesh,
        in_specs=placed,
        out_specs=(P("ctx", "tp"), P("ctx", "tp")),
        check_vma=False,
    )
```
